512 devices in a mesh: span: 8 (over y, x_lo), ctx: 64 (over x_hi, z, core).
Axes of the slice: x: 4 (x_hi: 2, x_lo: 2; x = x_hi * 2 + x_lo), y: 4, z: 16, core: 2. Of those that a mesh axis runs over, the one named last changes fastest.
Arguments:
- queries: bfloat16 [8, 1024, 8192], P('span', 'ctx'), may hold values from -120 to 120
- keys: bfloat16 [8, 1024, 8192], P('span', 'ctx'), may hold values from -6 to 6
- values: bfloat16 [8, 1024, 8192], P('span', 'ctx'), may hold values from -6 to 6
- span_mask: int32 [8, 8], replicated, may hold values from 0 to 1, as said below
- span_counts: int32 [8], replicated, may hold values from 768 to 1024, as said below
Outputs:
- attended: bfloat16 [8, 1024, 8192], P('span', 'ctx')
The draws below stay inside these ranges and needn't reach their ends.
Inputs may be any that keep to these rules, and one draw needn't show every extreme that they name: span_mask[i, i] is 1; span_mask[i, j] is 1 only for spans j that come before i in the denoising order, which is a permutation of the 8 spans. `span_counts`: some span is full.
All inputs are finite; a program needn't handle non-finite values.
Results may differ from the reference program's by a relative error of at most 0.02.
Values may be sent and summed in bfloat16 or wider, within the bound.
No kernel may reach another device: no remote copies, remote signals or barrier semaphores. Data moves between devices by JAX's collectives and lax.ppermute only.
A program may use at most 128 MiB of HBM per device.

```python
import jax
import jax.numpy as jnp
from jax import lax

HD = 128
HEADS = 64
SPAN_TOK = 1024
SPANS = 8


def shared_keys(key):
    base = jax.random.normal(jax.random.fold_in(key, 11), (SPANS, SPAN_TOK, HEADS * HD), jnp.float32)
    return jnp.clip(base, -6.0, 6.0)


def shared_order(key):
    return jax.random.permutation(jax.random.fold_in(key, 13), SPANS)


def draw_keys(key, part):
    common = shared_keys(key)
    return common.astype(jnp.bfloat16)


def draw_queries(key, part):
    key = jax.random.fold_in(key, 2)
    fresh = jnp.clip(jax.random.normal(key, (SPANS, SPAN_TOK, HEADS * HD), jnp.float32), -6.0, 6.0)
    return fresh.astype(jnp.bfloat16)


def draw_span_mask(key, part):
    order = shared_order(key)
    key = jax.random.fold_in(key, 3)
    coins = jax.random.randint(key, (SPANS, SPANS), 0, 4) > 0
    earlier = order[None, :] < order[:, None]
    same = jnp.eye(SPANS, dtype=bool)
    return (earlier & coins | same).astype(jnp.int32)


def draw_span_counts(key, part):
    key = jax.random.fold_in(key, 4)
    short = jax.random.randint(key, (SPANS,), 0, SPAN_TOK // 4 + 1)
    full = jax.random.randint(jax.random.fold_in(key, 1), (), 0, SPANS)
    counts = jnp.where(jnp.arange(SPANS) == full, 0, short)
    return (SPAN_TOK - counts).astype(jnp.int32)


def block_levels(stream_key, extent, shards, least, top_value):
    loudness, own = 1.0, jax.random.fold_in(stream_key, 6)
    for dim, shards_of in shards:
        steps = jnp.exp(jax.random.uniform(jax.random.fold_in(own, dim), (shards_of,), jnp.float32, least / len(shards), top_value / len(shards)))
        loudness = loudness * jnp.repeat(steps, extent[dim] // shards_of).reshape([-1 if axis == dim else 1 for axis in range(len(extent))])
    return loudness


def noise(stream_key, shape, spread, bound, cuts=(), kind=jnp.bfloat16):
    array = jax.random.normal(stream_key, shape, jnp.float32) * spread
    if len(cuts) > 0:
        array = block_levels(stream_key, shape, cuts, -0.22, 0.18) * array
    return jnp.clip(array, min=-bound, max=bound).astype(kind)


def setup_inputs(seed: int = 0) -> dict:
    splits = jax.random.split(jax.random.key(seed), 6)
    return {
        "queries": draw_queries(jax.random.fold_in(splits[5], 71), 0),
        "keys": draw_keys(jax.random.fold_in(splits[5], 71), 0),
        "values": noise(splits[2], (SPANS, SPAN_TOK, HEADS * HD), 1.0, 6.0, ((0, 8), (1, 64))),
        "span_mask": draw_span_mask(jax.random.fold_in(splits[5], 71), 0),
        "span_counts": draw_span_counts(jax.random.fold_in(splits[5], 71), 0),
    }


def reference(queries, keys, values, span_mask, span_counts):
    scale = 1.0 / (HD ** 0.5)
    q_heads = queries.reshape(SPANS, SPAN_TOK, HEADS, HD).transpose(0, 2, 1, 3)
    k_heads = keys.reshape(SPANS * SPAN_TOK, HEADS, HD).transpose(1, 0, 2)
    v_heads = values.reshape(SPANS * SPAN_TOK, HEADS, HD).transpose(1, 0, 2)
    slots = jnp.arange(SPANS * SPAN_TOK, dtype=jnp.int32)
    key_span = slots // SPAN_TOK
    key_live = (slots % SPAN_TOK) < span_counts[key_span]

    def single(pair):
        which = pair // HEADS
        head = pair % HEADS
        query = q_heads[which, head]
        score = jnp.dot(query, k_heads[head].T, preferred_element_type=jnp.float32) * scale
        keep = (span_mask[which][key_span] == 1) & key_live
        score = jnp.where(keep[None, :], score, -1e30)
        top = jnp.max(score, axis=1, keepdims=True)
        weight = jnp.where(keep[None, :], jnp.exp(score - top), 0.0)
        total = jnp.sum(weight, axis=1, keepdims=True)
        mixed = jnp.dot(weight.astype(jnp.bfloat16), v_heads[head], preferred_element_type=jnp.float32)
        return (mixed / total).astype(jnp.bfloat16)

    result = lax.map(single, jnp.arange(SPANS * HEADS, dtype=jnp.int32))
    result = result.reshape(SPANS, HEADS, SPAN_TOK, HD).transpose(0, 2, 1, 3)
    return result.reshape(SPANS, SPAN_TOK, HEADS * HD)
```

```python
import jax
import jax.numpy as jnp
from jax import lax
from jax.experimental import pallas as pl
from jax.experimental.pallas import tpu as pltpu
from jax.sharding import Mesh, PartitionSpec as P

HD = 128
LOW = -1e30


def attend_kernel(place, mask, counts, q_ref, *rest):
    pieces = rest[:8]
    out_ref, k_buf, v_buf, acc_ref, top_ref, total_ref, sems = rest[8:]
    x_lo, x_hi, core = place[0], place[1], place[2]
    x = x_hi * 2 + x_lo
    copies = []
    for d in range(4):
        from_hi = ((x + d) % 4) // 2
        for e in range(2):
            piece = pieces[2 * d + e]
            from_core = (core + e) % 2
            copies.append(
                pltpu.make_async_copy(
                    piece.at[:, 0], k_buf.at[d % 2, from_hi, from_core], sems.at[2 * d + e, 0]
                )
            )
            copies.append(
                pltpu.make_async_copy(
                    piece.at[:, 1], v_buf.at[d % 2, from_hi, from_core], sems.at[2 * d + e, 1]
                )
            )
    for copy in copies:
        copy.start()
    for copy in copies:
        copy.wait()

    scale = 1.0 / HD**0.5
    lane = lax.broadcasted_iota(jnp.int32, (1, 512), 1)
    slot = 512 + (lane % 256) // 16 * 32 + lane // 256 * 16 + lane % 16

    def query_block(iy, _):
        top_ref[...] = jnp.full_like(top_ref, LOW)
        total_ref[...] = jnp.zeros_like(total_ref)
        acc_ref[...] = jnp.zeros_like(acc_ref)
        span = iy * 2 + x_lo

        def key_block(block, _):
            rel, jy = block // 4, block % 4
            key_span = jy * 2 + (x_lo + rel) % 2

            @pl.when(mask[span, key_span] == 1)
            def _():
                q = q_ref[pl.ds(iy * 16, 16)].reshape(256, HD)
                k = k_buf[rel, :, :, pl.ds(jy * 16, 16)].reshape(1024, HD)
                v = v_buf[rel, :, :, pl.ds(jy * 16, 16)].reshape(1024, HD)
                s = lax.dot_general(
                    q, k, (((1,), (1,)), ((), ())), preferred_element_type=jnp.float32
                )
                upper = jnp.where(slot < counts[key_span], s[:, 512:], LOW)
                s = jnp.concatenate([s[:, :512], upper], axis=1)
                old = top_ref[...]
                top = jnp.maximum(old, jnp.max(s, axis=1, keepdims=True))
                factor = jnp.exp((old - top) * scale)
                weight = jnp.exp((s - top[:, :1]) * scale)
                total_ref[...] = total_ref[...] * factor + jnp.sum(weight, axis=1, keepdims=True)
                top_ref[...] = top
                acc_ref[...] = acc_ref[...] * factor + jnp.dot(
                    weight.astype(jnp.bfloat16), v, preferred_element_type=jnp.float32
                )

            return 0

        lax.fori_loop(0, 8, key_block, 0)
        result = acc_ref[...] / total_ref[...]
        out_ref[pl.ds(iy * 16, 16)] = result.astype(jnp.bfloat16).reshape(16, 16, HD)
        return 0

    lax.fori_loop(0, 4, query_block, 0)


def attend(place, mask, counts, q, pieces):
    smem = pl.BlockSpec(memory_space=pltpu.SMEM)
    vmem = pl.BlockSpec(memory_space=pltpu.VMEM)
    return pl.pallas_call(
        attend_kernel,
        out_shape=jax.ShapeDtypeStruct(q.shape, jnp.bfloat16),
        in_specs=[smem, smem, smem, vmem] + [pl.BlockSpec(memory_space=pl.ANY)] * 8,
        out_specs=vmem,
        scratch_shapes=[
            pltpu.VMEM((2, 2, 2, 64, 16, HD), jnp.bfloat16),
            pltpu.VMEM((2, 2, 2, 64, 16, HD), jnp.bfloat16),
            pltpu.VMEM((256, HD), jnp.float32),
            pltpu.VMEM((256, HD), jnp.float32),
            pltpu.VMEM((256, HD), jnp.float32),
            pltpu.SemaphoreType.DMA((8, 2)),
        ],
        compiler_params=pltpu.CompilerParams(vmem_limit_bytes=40 * 1024 * 1024),
        cost_estimate=pl.CostEstimate(
            flops=4 * 1024 * 8192 * HD, bytes_accessed=5 << 20, transcendentals=1024 * 8192
        ),
    )(place, mask, counts, q, *pieces)


def ring(step):
    def index(x):
        return (x % 2) * 2 + x // 2

    return [(index(x), index((x + step) % 4)) for x in range(4)]


def per_device(queries, keys, values, span_mask, span_counts):
    tok_rows, width = queries.shape[1], queries.shape[2]
    heads = width // HD

    def by_head(array):
        return array.reshape(tok_rows, heads, HD).transpose(1, 0, 2)

    def exchange(array):
        return lax.all_to_all(array, ("y", "z"), split_axis=0, concat_axis=0, tiled=True)

    kv = exchange(jnp.stack([by_head(keys), by_head(values)], axis=1))
    q_in, kv = lax.optimization_barrier((by_head(queries), kv))
    q = exchange(q_in)

    x_axes = ("x_lo", "x_hi")
    swap = [(0, 1), (1, 0)]
    own = [
        kv,
        lax.ppermute(kv, x_axes, ring(-1)),
        lax.ppermute(kv, x_axes, ring(2)),
        lax.ppermute(kv, x_axes, ring(1)),
    ]
    pieces = []
    for piece in own:
        pieces += [piece, lax.ppermute(piece, "core", swap)]
    place = jnp.stack([lax.axis_index("x_lo"), lax.axis_index("x_hi"), lax.axis_index("core")])
    out = attend(place.astype(jnp.int32), span_mask, span_counts, q, pieces)
    back = exchange(out)
    return back.transpose(1, 0, 2).reshape(1, tok_rows, width)


def solution(mesh):
    fine = Mesh(mesh.devices.reshape(4, 2, 2, 16, 2), ("y", "x_lo", "x_hi", "z", "core"))
    split = P(("y", "x_lo"), ("x_hi", "z", "core"), None)
    return jax.shard_map(
        per_device,
        mesh=fine,
        in_specs=(split, split, split, P(), P()),
        out_specs=split,
        check_vma=False,
    )
```

```python
import jax
import jax.numpy as jnp
from jax import lax
from jax.experimental import pallas as pl
from jax.experimental.pallas import tpu as pltpu
from jax.sharding import Mesh, PartitionSpec as P

HD = 128
LOW = -1e30
LOG2E = 1.4426950408889634


def attend_kernel(place, mask, counts, q_ref, *rest):
    pieces = rest[:8]
    out_ref, k_buf, v_buf, s_a, s_b, m_a, m_b, acc_ref, top_ref, total_ref, todo, sems = rest[8:]
    scores, row_tops = (s_a, s_b), (m_a, m_b)
    x_lo, x_hi, core = place[0], place[1], place[2]
    x = x_hi * 2 + x_lo
    copies = {}
    for d in (0, 2, 1, 3):
        for part, buf in enumerate((k_buf, v_buf)):
            for e in range(2):
                copies[d, e, part] = pltpu.make_async_copy(
                    pieces[2 * d + e].at[:, part],
                    buf.at[d % 2, ((x + d) % 4) // 2, (core + e) % 2],
                    sems.at[2 * d + e, part],
                )
    for side in range(2):
        for part in range(2):
            for d in (side, side + 2):
                for e in range(2):
                    copies[d, e, part].start()

    def wait(side, part):
        for d in (side, side + 2):
            for e in range(2):
                copies[d, e, part].wait()

    def list_block(i, n):
        side, iy, jy = i // 16, i // 4 % 4, i % 4
        todo[n] = i
        return n + mask[iy * 2 + x_lo, jy * 2 + (x_lo + side) % 2]

    near = lax.fori_loop(0, 16, list_block, 0)
    count = lax.fori_loop(16, 32, list_block, near)

    acc_ref[...] = jnp.zeros_like(acc_ref)
    top_ref[...] = jnp.full_like(top_ref, LOW)
    total_ref[...] = jnp.zeros_like(total_ref)
    scale = LOG2E / HD**0.5
    lane = lax.broadcasted_iota(jnp.int32, (1, 128), 1)
    late = 768 + lane // 16 * 32 + lane % 16

    def score(n, slot):
        i = todo[n]
        side, iy, jy = i // 16, i // 4 % 4, i % 4
        live = counts[jy * 2 + (x_lo + side) % 2]
        q = q_ref[pl.ds(iy * 16, 16)].reshape(256, HD)
        top = None
        for hi in range(2):
            for c in range(2):
                k = k_buf[side, hi, c, pl.ds(jy * 16, 16)].reshape(256, HD)
                s = lax.dot_general(q, k, (((1,), (1,)), ((), ())), preferred_element_type=jnp.float32)
                a, b = s[:, :128], s[:, 128:]
                if hi == 1:
                    b = jnp.where(late + c * 16 < live, b, LOW)
                at = (hi * 2 + c) * 256
                scores[slot][:, at : at + 128] = a
                scores[slot][:, at + 128 : at + 256] = b
                both = jnp.maximum(a, b)
                top = both if top is None else jnp.maximum(top, both)
        row_tops[slot][...] = jnp.broadcast_to(jnp.max(top, axis=1, keepdims=True), (256, 128))

    def half(n, slot):
        i = todo[n]
        side, iy, jy = i // 16, i // 4 % 4, i % 4

        @pl.when(n + 1 == near)
        def _():
            wait(1, 0)
            wait(1, 1)
        old = top_ref[iy]
        top = jnp.maximum(old, row_tops[slot][...])
        shift = top * scale
        factor = jnp.exp2(old * scale - shift)
        total = total_ref[iy] * factor
        acc = acc_ref[iy] * factor
        score(jnp.minimum(n + 1, count - 1), 1 - slot)
        for g in range(4):
            at = g * 256
            wa = jnp.exp2(scores[slot][:, at : at + 128] * scale - shift)
            wb = jnp.exp2(scores[slot][:, at + 128 : at + 256] * scale - shift)
            total = total + wa + wb
            w = jnp.concatenate([wa.astype(jnp.bfloat16), wb.astype(jnp.bfloat16)], axis=1)
            v = v_buf[side, g // 2, g % 2, pl.ds(jy * 16, 16)].reshape(256, HD)
            acc = acc + jnp.dot(w, v, preferred_element_type=jnp.float32)
        total_ref[iy] = total
        top_ref[iy] = top
        acc_ref[iy] = acc

    wait(0, 0)
    score(0, 0)
    wait(0, 1)

    def pair(n, _):
        half(2 * n, 0)

        @pl.when(2 * n + 1 < count)
        def _():
            half(2 * n + 1, 1)

        return 0

    lax.fori_loop(0, (count + 1) // 2, pair, 0)
    for iy in range(4):
        total = jnp.sum(total_ref[iy], axis=1, keepdims=True)
        out_ref[iy * 16 : (iy + 1) * 16] = (acc_ref[iy] / total).astype(jnp.bfloat16).reshape(16, 16, HD)

def attend(place, mask, counts, q, pieces):
    smem = pl.BlockSpec(memory_space=pltpu.SMEM)
    vmem = pl.BlockSpec(memory_space=pltpu.VMEM)
    return pl.pallas_call(
        attend_kernel,
        out_shape=jax.ShapeDtypeStruct(q.shape, jnp.bfloat16),
        in_specs=[smem, smem, smem, vmem] + [pl.BlockSpec(memory_space=pl.ANY)] * 8,
        out_specs=vmem,
        scratch_shapes=[
            pltpu.VMEM((2, 2, 2, 64, 16, HD), jnp.bfloat16),
            pltpu.VMEM((2, 2, 2, 64, 16, HD), jnp.bfloat16),
            pltpu.VMEM((256, 1024), jnp.float32),
            pltpu.VMEM((256, 1024), jnp.float32),
            pltpu.VMEM((256, HD), jnp.float32),
            pltpu.VMEM((256, HD), jnp.float32),
            pltpu.VMEM((4, 256, HD), jnp.float32),
            pltpu.VMEM((4, 256, HD), jnp.float32),
            pltpu.VMEM((4, 256, HD), jnp.float32),
            pltpu.SMEM((33,), jnp.int32),
            pltpu.SemaphoreType.DMA((8, 2)),
        ],
        compiler_params=pltpu.CompilerParams(vmem_limit_bytes=40 * 1024 * 1024),
        cost_estimate=pl.CostEstimate(
            flops=4 * 1024 * 8192 * HD, bytes_accessed=5 << 20, transcendentals=1024 * 8192
        ),
    )(place, mask, counts, q, *pieces)


def ring(step):
    def index(x):
        return (x % 2) * 2 + x // 2

    return [(index(x), index((x + step) % 4)) for x in range(4)]


def per_device(queries, keys, values, span_mask, span_counts):
    tok_rows, width = queries.shape[1], queries.shape[2]
    heads = width // HD

    def by_head(array):
        return array.reshape(tok_rows, heads, HD).transpose(1, 0, 2)

    def exchange(array):
        return lax.all_to_all(array, ("y", "z"), split_axis=0, concat_axis=0, tiled=True)

    kv = exchange(jnp.stack([by_head(keys), by_head(values)], axis=1))
    q_in, kv = lax.optimization_barrier((by_head(queries), kv))
    q = exchange(q_in)

    def gather(kv):
        x_axes = ("x_lo", "x_hi")
        swap = [(0, 1), (1, 0)]
        ahead, back, far = [lax.ppermute(kv, x_axes, ring(step)) for step in (-1, 1, 2)]
        other = [lax.ppermute(piece, "core", swap) for piece in (kv, ahead, back, far)]
        return [other[0], ahead, other[1], far, other[3], back, other[2]]

    def gather_own(kv):
        x_axes = ("x_lo", "x_hi")
        swap = [(0, 1), (1, 0)]
        far = lax.ppermute(kv, x_axes, ring(2))
        other = lax.ppermute(kv, "core", swap)
        return [other, kv, other, far, lax.ppermute(far, "core", swap), kv, other]

    crossing = jnp.sum(span_mask) > span_mask.shape[0]
    pieces = [kv] + lax.cond(crossing, gather, gather_own, kv)
    place = jnp.stack([lax.axis_index("x_lo"), lax.axis_index("x_hi"), lax.axis_index("core")])
    out = attend(place.astype(jnp.int32), span_mask, span_counts, q, pieces)
    back = exchange(out)
    return back.transpose(1, 0, 2).reshape(1, tok_rows, width)


def solution(mesh):
    fine = Mesh(mesh.devices.reshape(4, 2, 2, 16, 2), ("y", "x_lo", "x_hi", "z", "core"))
    split = P(("y", "x_lo"), ("x_hi", "z", "core"), None)
    return jax.shard_map(
        per_device,
        mesh=fine,
        in_specs=(split, split, split, P(), P()),
        out_specs=split,
        check_vma=False,
    )
```

```python
import jax
import jax.numpy as jnp
from jax import lax
from jax.experimental import pallas as pl
from jax.experimental.pallas import tpu as pltpu
from jax.sharding import Mesh, PartitionSpec as P

HD = 128
LOW = -1e30
LOG2E = 1.4426950408889634


def attend_kernel(place, mask, counts, q_ref, *rest):
    near, far = rest[:6], rest[6:10]
    out_ref, k_buf, v_buf, s_a, s_b, m_a, m_b, acc_ref, top_ref, total_ref, todo, sems = rest[10:]
    scores, row_tops = (s_a, s_b), (m_a, m_b)
    x_lo, x_hi, core = place[0], place[1], place[2]
    x = x_hi * 2 + x_lo
    copies = {}
    for d in range(4):
        for part, buf in enumerate((k_buf, v_buf)):
            for e in range(2):
                copies[d, e, part] = pltpu.make_async_copy(
                    far[2 * part + e] if d == 2 else near[2 * (d - d // 3) + e].at[:, part],
                    buf.at[d % 2, ((x + d) % 4) // 2, (core + e) % 2],
                    sems.at[2 * d + e, part],
                )
    for side in range(2):
        for part in range(2):
            for d in (side, side + 2):
                for e in range(2):
                    copies[d, e, part].start()

    def wait(side, part):
        for d in (side, side + 2):
            for e in range(2):
                copies[d, e, part].wait()

    def list_block(i, n):
        side, iy, jy = i // 16, i // 4 % 4, i % 4
        todo[n] = i
        return n + mask[iy * 2 + x_lo, jy * 2 + (x_lo + side) % 2]

    first = lax.fori_loop(0, 16, list_block, 0)
    count = lax.fori_loop(16, 32, list_block, first)

    acc_ref[...] = jnp.zeros_like(acc_ref)
    top_ref[...] = jnp.full_like(top_ref, LOW)
    total_ref[...] = jnp.zeros_like(total_ref)
    scale = LOG2E / HD**0.5
    lane = lax.broadcasted_iota(jnp.int32, (1, 128), 1)
    late = 768 + lane // 16 * 32 + lane % 16

    def score(n, slot):
        i = todo[n]
        side, iy, jy = i // 16, i // 4 % 4, i % 4
        live = counts[jy * 2 + (x_lo + side) % 2]
        q = q_ref[pl.ds(iy * 16, 16)].reshape(256, HD)
        top = None
        for hi in range(2):
            for c in range(2):
                k = k_buf[side, hi, c, pl.ds(jy * 16, 16)].reshape(256, HD)
                s = lax.dot_general(q, k, (((1,), (1,)), ((), ())), preferred_element_type=jnp.float32)
                a, b = s[:, :128], s[:, 128:]
                if hi == 1:
                    b = jnp.where(late + c * 16 < live, b, LOW)
                at = (hi * 2 + c) * 256
                scores[slot][:, at : at + 128] = a
                scores[slot][:, at + 128 : at + 256] = b
                both = jnp.maximum(a, b)
                top = both if top is None else jnp.maximum(top, both)
        row_tops[slot][...] = jnp.broadcast_to(jnp.max(top, axis=1, keepdims=True), (256, 128))

    def half(n, slot):
        i = todo[n]
        side, iy, jy = i // 16, i // 4 % 4, i % 4

        @pl.when(n + 1 == first)
        def _():
            wait(1, 0)
            wait(1, 1)
        old = top_ref[iy]
        top = jnp.maximum(old, row_tops[slot][...])
        shift = top * scale
        factor = jnp.exp2(old * scale - shift)
        total = total_ref[iy] * factor
        acc = acc_ref[iy] * factor
        score(jnp.minimum(n + 1, count - 1), 1 - slot)
        for g in range(4):
            at = g * 256
            wa = jnp.exp2(scores[slot][:, at : at + 128] * scale - shift)
            wb = jnp.exp2(scores[slot][:, at + 128 : at + 256] * scale - shift)
            total = total + wa + wb
            w = jnp.concatenate([wa.astype(jnp.bfloat16), wb.astype(jnp.bfloat16)], axis=1)
            v = v_buf[side, g // 2, g % 2, pl.ds(jy * 16, 16)].reshape(256, HD)
            acc = acc + jnp.dot(w, v, preferred_element_type=jnp.float32)
        total_ref[iy] = total
        top_ref[iy] = top
        acc_ref[iy] = acc

    wait(0, 0)
    score(0, 0)
    wait(0, 1)

    def pair(n, _):
        half(2 * n, 0)

        @pl.when(2 * n + 1 < count)
        def _():
            half(2 * n + 1, 1)

        return 0

    lax.fori_loop(0, (count + 1) // 2, pair, 0)
    for iy in range(4):
        total = jnp.sum(total_ref[iy], axis=1, keepdims=True)
        out_ref[iy * 16 : (iy + 1) * 16] = (acc_ref[iy] / total).astype(jnp.bfloat16).reshape(16, 16, HD)

def attend(place, mask, counts, q, near, far):
    smem = pl.BlockSpec(memory_space=pltpu.SMEM)
    vmem = pl.BlockSpec(memory_space=pltpu.VMEM)
    return pl.pallas_call(
        attend_kernel,
        out_shape=jax.ShapeDtypeStruct(q.shape, jnp.bfloat16),
        in_specs=[smem, smem, smem, vmem] + [pl.BlockSpec(memory_space=pl.ANY)] * 10,
        out_specs=vmem,
        scratch_shapes=[
            pltpu.VMEM((2, 2, 2, 64, 16, HD), jnp.bfloat16),
            pltpu.VMEM((2, 2, 2, 64, 16, HD), jnp.bfloat16),
            pltpu.VMEM((256, 1024), jnp.float32),
            pltpu.VMEM((256, 1024), jnp.float32),
            pltpu.VMEM((256, HD), jnp.float32),
            pltpu.VMEM((256, HD), jnp.float32),
            pltpu.VMEM((4, 256, HD), jnp.float32),
            pltpu.VMEM((4, 256, HD), jnp.float32),
            pltpu.VMEM((4, 256, HD), jnp.float32),
            pltpu.SMEM((33,), jnp.int32),
            pltpu.SemaphoreType.DMA((8, 2)),
        ],
        compiler_params=pltpu.CompilerParams(vmem_limit_bytes=40 * 1024 * 1024),
        cost_estimate=pl.CostEstimate(
            flops=4 * 1024 * 8192 * HD, bytes_accessed=5 << 20, transcendentals=1024 * 8192
        ),
    )(place, mask, counts, q, *near, *far)


def pack_kernel(k_ref, v_ref, out_ref):
    for head in range(out_ref.shape[0]):
        at = head * HD
        out_ref[head, 0] = k_ref[:, at : at + HD]
        out_ref[head, 1] = v_ref[:, at : at + HD]


def pack(keys, values):
    rows, width = keys.shape
    return pl.pallas_call(
        pack_kernel,
        out_shape=jax.ShapeDtypeStruct((width // HD, 2, rows, HD), keys.dtype),
        in_specs=[pl.BlockSpec(memory_space=pltpu.VMEM)] * 2,
        out_specs=pl.BlockSpec(memory_space=pltpu.VMEM),
    )(keys, values)


def ring(step):
    def index(x):
        return (x % 2) * 2 + x // 2

    return [(index(x), index((x + step) % 4)) for x in range(4)]


def per_device(queries, keys, values, span_mask, span_counts):
    tok_rows, width = queries.shape[1], queries.shape[2]
    heads = width // HD

    def by_head(array):
        return array.reshape(tok_rows, heads, HD).transpose(1, 0, 2)

    def exchange(array):
        return lax.all_to_all(array, ("y", "z"), split_axis=0, concat_axis=0, tiled=True)

    kv = exchange(pack(keys[0], values[0]))
    q_in, kv = lax.optimization_barrier((by_head(queries), kv))
    q = exchange(q_in)

    x_axes = ("x_lo", "x_hi")

    def with_other_core(piece):
        return [piece, lax.ppermute(piece, "core", [(0, 1), (1, 0)])]

    near = with_other_core(kv)
    for step in (-1, 1):
        near += with_other_core(lax.ppermute(kv, x_axes, ring(step)))
    far = []
    for part in range(2):
        far += with_other_core(lax.ppermute(kv[:, part], x_axes, ring(2)))
    place = jnp.stack([lax.axis_index("x_lo"), lax.axis_index("x_hi"), lax.axis_index("core")])
    out = attend(place.astype(jnp.int32), span_mask, span_counts, q, near, far)
    back = exchange(out)
    return back.transpose(1, 0, 2).reshape(1, tok_rows, width)


def solution(mesh):
    fine = Mesh(mesh.devices.reshape(4, 2, 2, 16, 2), ("y", "x_lo", "x_hi", "z", "core"))
    split = P(("y", "x_lo"), ("x_hi", "z", "core"), None)
    return jax.shard_map(
        per_device,
        mesh=fine,
        in_specs=(split, split, split, P(), P()),
        out_specs=split,
        check_vma=False,
    )
```

```python
import jax
import jax.numpy as jnp
from jax import lax
from jax.experimental import pallas as pl
from jax.experimental.pallas import tpu as pltpu
from jax.sharding import Mesh, PartitionSpec as P

HD = 128
LOW = -1e30
LOG2E = 1.4426950408889634


def attend_kernel(place, mask, counts, q_ref, *rest):
    pieces = rest[:8]
    out_ref, k_buf, v_buf, s_a, s_b, m_a, m_b, acc_ref, top_ref, total_ref, todo, sems = rest[8:]
    scores, row_tops = (s_a, s_b), (m_a, m_b)
    x_lo, x_hi, core = place[0], place[1], place[2]
    x = x_hi * 2 + x_lo
    copies = {}
    for d in range(4):
        for part, buf in enumerate((k_buf, v_buf)):
            for e in range(2):
                copies[d, e, part] = pltpu.make_async_copy(
                    pieces[2 * d + e].at[:, part],
                    buf.at[d % 2, ((x + d) % 4) // 2, (core + e) % 2],
                    sems.at[2 * d + e, part],
                )
    for side in range(2):
        for part in range(2):
            for d in (side, side + 2):
                for e in range(2):
                    copies[d, e, part].start()

    def wait(side, part):
        for d in (side, side + 2):
            for e in range(2):
                copies[d, e, part].wait()

    def list_block(i, n):
        side, iy, jy = i // 16, i // 4 % 4, i % 4
        todo[n] = i
        return n + mask[iy * 2 + x_lo, jy * 2 + (x_lo + side) % 2]

    first = lax.fori_loop(0, 16, list_block, 0)
    count = lax.fori_loop(16, 32, list_block, first)

    acc_ref[...] = jnp.zeros_like(acc_ref)
    top_ref[...] = jnp.full_like(top_ref, LOW)
    total_ref[...] = jnp.zeros_like(total_ref)
    scale = LOG2E / HD**0.5
    lane = lax.broadcasted_iota(jnp.int32, (1, 128), 1)
    late = 768 + lane // 16 * 32 + lane % 16

    def score(n, slot):
        i = todo[n]
        side, iy, jy = i // 16, i // 4 % 4, i % 4
        live = counts[jy * 2 + (x_lo + side) % 2]
        q = q_ref[pl.ds(iy * 16, 16)].reshape(256, HD)
        top = None
        for hi in range(2):
            for c in range(2):
                k = k_buf[side, hi, c, pl.ds(jy * 16, 16)].reshape(256, HD)
                s = lax.dot_general(q, k, (((1,), (1,)), ((), ())), preferred_element_type=jnp.float32)
                a, b = s[:, :128], s[:, 128:]
                if hi == 1:
                    b = jnp.where(late + c * 16 < live, b, LOW)
                at = (hi * 2 + c) * 256
                scores[slot][:, at : at + 128] = a
                scores[slot][:, at + 128 : at + 256] = b
                both = jnp.maximum(a, b)
                top = both if top is None else jnp.maximum(top, both)
        row_tops[slot][...] = jnp.broadcast_to(jnp.max(top, axis=1, keepdims=True), (256, 128))

    def half(n, slot):
        i = todo[n]
        side, iy, jy = i // 16, i // 4 % 4, i % 4

        @pl.when(n + 1 == first)
        def _():
            wait(1, 0)
            wait(1, 1)
        old = top_ref[iy]
        top = jnp.maximum(old, row_tops[slot][...])
        shift = top * scale
        factor = jnp.exp2(old * scale - shift)
        total = total_ref[iy] * factor
        acc = acc_ref[iy] * factor
        score(jnp.minimum(n + 1, count - 1), 1 - slot)
        for g in range(4):
            at = g * 256
            wa = jnp.exp2(scores[slot][:, at : at + 128] * scale - shift)
            wb = jnp.exp2(scores[slot][:, at + 128 : at + 256] * scale - shift)
            total = total + wa + wb
            w = jnp.concatenate([wa.astype(jnp.bfloat16), wb.astype(jnp.bfloat16)], axis=1)
            v = v_buf[side, g // 2, g % 2, pl.ds(jy * 16, 16)].reshape(256, HD)
            acc = acc + jnp.dot(w, v, preferred_element_type=jnp.float32)
        total_ref[iy] = total
        top_ref[iy] = top
        acc_ref[iy] = acc

    wait(0, 0)
    score(0, 0)
    wait(0, 1)

    def pair(n, _):
        half(2 * n, 0)

        @pl.when(2 * n + 1 < count)
        def _():
            half(2 * n + 1, 1)

        return 0

    lax.fori_loop(0, (count + 1) // 2, pair, 0)
    for iy in range(4):
        total = jnp.sum(total_ref[iy], axis=1, keepdims=True)
        out_ref[iy * 16 : (iy + 1) * 16] = (acc_ref[iy] / total).astype(jnp.bfloat16).reshape(16, 16, HD)

def attend(place, mask, counts, q, pieces):
    smem = pl.BlockSpec(memory_space=pltpu.SMEM)
    vmem = pl.BlockSpec(memory_space=pltpu.VMEM)
    return pl.pallas_call(
        attend_kernel,
        out_shape=jax.ShapeDtypeStruct(q.shape, jnp.bfloat16),
        in_specs=[smem, smem, smem, vmem] + [pl.BlockSpec(memory_space=pl.ANY)] * 8,
        out_specs=vmem,
        scratch_shapes=[
            pltpu.VMEM((2, 2, 2, 64, 16, HD), jnp.bfloat16),
            pltpu.VMEM((2, 2, 2, 64, 16, HD), jnp.bfloat16),
            pltpu.VMEM((256, 1024), jnp.float32),
            pltpu.VMEM((256, 1024), jnp.float32),
            pltpu.VMEM((256, HD), jnp.float32),
            pltpu.VMEM((256, HD), jnp.float32),
            pltpu.VMEM((4, 256, HD), jnp.float32),
            pltpu.VMEM((4, 256, HD), jnp.float32),
            pltpu.VMEM((4, 256, HD), jnp.float32),
            pltpu.SMEM((33,), jnp.int32),
            pltpu.SemaphoreType.DMA((8, 2)),
        ],
        compiler_params=pltpu.CompilerParams(vmem_limit_bytes=40 * 1024 * 1024),
        cost_estimate=pl.CostEstimate(
            flops=4 * 1024 * 8192 * HD, bytes_accessed=5 << 20, transcendentals=1024 * 8192
        ),
    )(place, mask, counts, q, *pieces)


def pack_kernel(k_ref, v_ref, out_ref):
    for head in range(out_ref.shape[0]):
        at = head * HD
        out_ref[head, 0] = k_ref[:, at : at + HD]
        out_ref[head, 1] = v_ref[:, at : at + HD]


def pack(keys, values):
    rows, width = keys.shape
    return pl.pallas_call(
        pack_kernel,
        out_shape=jax.ShapeDtypeStruct((width // HD, 2, rows, HD), keys.dtype),
        in_specs=[pl.BlockSpec(memory_space=pltpu.VMEM)] * 2,
        out_specs=pl.BlockSpec(memory_space=pltpu.VMEM),
    )(keys, values)


def ring(step):
    def index(x):
        return (x % 2) * 2 + x // 2

    return [(index(x), index((x + step) % 4)) for x in range(4)]


def per_device(queries, keys, values, span_mask, span_counts):
    tok_rows, width = queries.shape[1], queries.shape[2]
    heads = width // HD

    def by_head(array):
        return array.reshape(tok_rows, heads, HD).transpose(1, 0, 2)

    def exchange(array):
        return lax.all_to_all(array, ("y", "z"), split_axis=0, concat_axis=0, tiled=True)

    kv = exchange(pack(keys[0], values[0]))
    q_in, kv = lax.optimization_barrier((by_head(queries), kv))
    q = exchange(q_in)

    x_axes = ("x_lo", "x_hi")
    pieces = []
    for piece in [kv] + [lax.ppermute(kv, x_axes, ring(step)) for step in (-1, 2, 1)]:
        pieces += [piece, lax.ppermute(piece, "core", [(0, 1), (1, 0)])]
    place = jnp.stack([lax.axis_index("x_lo"), lax.axis_index("x_hi"), lax.axis_index("core")])
    out = attend(place.astype(jnp.int32), span_mask, span_counts, q, pieces)
    back = exchange(out)
    return back.transpose(1, 0, 2).reshape(1, tok_rows, width)


def solution(mesh):
    fine = Mesh(mesh.devices.reshape(4, 2, 2, 16, 2), ("y", "x_lo", "x_hi", "z", "core"))
    split = P(("y", "x_lo"), ("x_hi", "z", "core"), None)
    return jax.shard_map(
        per_device,
        mesh=fine,
        in_specs=(split, split, split, P(), P()),
        out_specs=split,
        check_vma=False,
    )
```

```python
import jax
import jax.numpy as jnp
from jax import lax
from jax.experimental import pallas as pl
from jax.experimental.pallas import tpu as pltpu
from jax.sharding import Mesh, PartitionSpec as P

HD = 128
LOW = -1e30
LOG2E = 1.4426950408889634


def attend_kernel(place, mask, counts, q_ref, *rest):
    pieces = rest[:8]
    out_ref, k_buf, v_buf, s_a, s_b, m_a, m_b, acc_ref, top_ref, total_ref, todo, sems = rest[8:]
    scores, row_tops = (s_a, s_b), (m_a, m_b)
    x_lo, x_hi, core, y = place[0], place[1], place[2], place[3]
    x = x_hi * 2 + x_lo
    copies = {}
    for d in range(4):
        for part, buf in enumerate((k_buf, v_buf)):
            for e in range(2):
                copies[d, e, part] = pltpu.make_async_copy(
                    pieces[2 * d + e].at[:, part],
                    buf.at[d % 2, ((x + d) % 4) // 2, (core + e) % 2],
                    sems.at[2 * d + e, part],
                )
    for side in range(2):
        for part in range(2):
            for d in (side, side + 2):
                for e in range(2):
                    copies[d, e, part].start()

    def wait(side, part):
        for d in (side, side + 2):
            for e in range(2):
                copies[d, e, part].wait()

    def list_block(i, n):
        side, iy, jy = i // 16, i // 4 % 4, i % 4
        todo[n] = i
        return n + mask[iy * 2 + x_lo, jy * 2 + (x_lo + side) % 2]

    first = lax.fori_loop(0, 16, list_block, 0)
    count = lax.fori_loop(16, 32, list_block, first)

    acc_ref[...] = jnp.zeros_like(acc_ref)
    top_ref[...] = jnp.full_like(top_ref, LOW)
    total_ref[...] = jnp.zeros_like(total_ref)
    scale = LOG2E / HD**0.5
    lane = lax.broadcasted_iota(jnp.int32, (1, 128), 1)
    late = 768 + lane // 16 * 32 + lane % 16

    def score(n, slot):
        i = todo[n]
        side, iy, jy = i // 16, i // 4 % 4, i % 4
        live = counts[jy * 2 + (x_lo + side) % 2]
        q = q_ref[:, (y + 4 - iy) % 4].reshape(256, HD)
        top = None
        for hi in range(2):
            for c in range(2):
                k = k_buf[side, hi, c, pl.ds(jy * 16, 16)].reshape(256, HD)
                s = lax.dot_general(q, k, (((1,), (1,)), ((), ())), preferred_element_type=jnp.float32)
                a, b = s[:, :128], s[:, 128:]
                if hi == 1:
                    b = jnp.where(late + c * 16 < live, b, LOW)
                at = (hi * 2 + c) * 256
                scores[slot][:, at : at + 128] = a
                scores[slot][:, at + 128 : at + 256] = b
                both = jnp.maximum(a, b)
                top = both if top is None else jnp.maximum(top, both)
        row_tops[slot][...] = jnp.broadcast_to(jnp.max(top, axis=1, keepdims=True), (256, 128))

    def half(n, slot):
        i = todo[n]
        side, iy, jy = i // 16, i // 4 % 4, i % 4

        @pl.when(n + 1 == first)
        def _():
            wait(1, 0)
            wait(1, 1)
        old = top_ref[iy]
        top = jnp.maximum(old, row_tops[slot][...])
        shift = top * scale
        factor = jnp.exp2(old * scale - shift)
        total = total_ref[iy] * factor
        acc = acc_ref[iy] * factor
        score(jnp.minimum(n + 1, count - 1), 1 - slot)
        for g in range(4):
            at = g * 256
            wa = jnp.exp2(scores[slot][:, at : at + 128] * scale - shift)
            wb = jnp.exp2(scores[slot][:, at + 128 : at + 256] * scale - shift)
            total = total + wa + wb
            w = jnp.concatenate([wa.astype(jnp.bfloat16), wb.astype(jnp.bfloat16)], axis=1)
            v = v_buf[side, g // 2, g % 2, pl.ds(jy * 16, 16)].reshape(256, HD)
            acc = acc + jnp.dot(w, v, preferred_element_type=jnp.float32)
        total_ref[iy] = total
        top_ref[iy] = top
        acc_ref[iy] = acc

    wait(0, 0)
    score(0, 0)
    wait(0, 1)

    def pair(n, _):
        half(2 * n, 0)

        @pl.when(2 * n + 1 < count)
        def _():
            half(2 * n + 1, 1)

        return 0

    lax.fori_loop(0, (count + 1) // 2, pair, 0)
    for iy in range(4):
        total = jnp.sum(total_ref[iy], axis=1, keepdims=True)
        out_ref[iy * 16 : (iy + 1) * 16] = (acc_ref[iy] / total).astype(jnp.bfloat16).reshape(16, 16, HD)

def attend(place, mask, counts, q, pieces):
    smem = pl.BlockSpec(memory_space=pltpu.SMEM)
    vmem = pl.BlockSpec(memory_space=pltpu.VMEM)
    return pl.pallas_call(
        attend_kernel,
        out_shape=jax.ShapeDtypeStruct((64, 16, HD), jnp.bfloat16),
        in_specs=[smem, smem, smem, vmem] + [pl.BlockSpec(memory_space=pl.ANY)] * 8,
        out_specs=vmem,
        scratch_shapes=[
            pltpu.VMEM((2, 2, 2, 64, 16, HD), jnp.bfloat16),
            pltpu.VMEM((2, 2, 2, 64, 16, HD), jnp.bfloat16),
            pltpu.VMEM((256, 1024), jnp.float32),
            pltpu.VMEM((256, 1024), jnp.float32),
            pltpu.VMEM((256, HD), jnp.float32),
            pltpu.VMEM((256, HD), jnp.float32),
            pltpu.VMEM((4, 256, HD), jnp.float32),
            pltpu.VMEM((4, 256, HD), jnp.float32),
            pltpu.VMEM((4, 256, HD), jnp.float32),
            pltpu.SMEM((33,), jnp.int32),
            pltpu.SemaphoreType.DMA((8, 2)),
        ],
        compiler_params=pltpu.CompilerParams(vmem_limit_bytes=40 * 1024 * 1024),
        cost_estimate=pl.CostEstimate(
            flops=4 * 1024 * 8192 * HD, bytes_accessed=5 << 20, transcendentals=1024 * 8192
        ),
    )(place, mask, counts, q, *pieces)


def pack_kernel(k_ref, v_ref, out_ref):
    for head in range(out_ref.shape[0]):
        at = head * HD
        out_ref[head, 0] = k_ref[:, at : at + HD]
        out_ref[head, 1] = v_ref[:, at : at + HD]


def pack(keys, values):
    rows, width = keys.shape
    return pl.pallas_call(
        pack_kernel,
        out_shape=jax.ShapeDtypeStruct((width // HD, 2, rows, HD), keys.dtype),
        in_specs=[pl.BlockSpec(memory_space=pltpu.VMEM)] * 2,
        out_specs=pl.BlockSpec(memory_space=pltpu.VMEM),
    )(keys, values)


def ring(step):
    def index(x):
        return (x % 2) * 2 + x // 2

    return [(index(x), index((x + step) % 4)) for x in range(4)]


def per_device(queries, keys, values, span_mask, span_counts):
    tok_rows, width = queries.shape[1], queries.shape[2]
    heads = width // HD

    def by_head(array):
        return array.reshape(tok_rows, heads, HD).transpose(1, 0, 2)

    def exchange(array):
        return lax.all_to_all(array, ("y", "z"), split_axis=0, concat_axis=0, tiled=True)

    kv = exchange(pack(keys[0], values[0]))
    n_y = lax.axis_size("y")
    y = lax.axis_index("y")
    by_group = by_head(queries).reshape(n_y, heads // n_y, tok_rows, HD)
    parts = []
    for d in range(n_y):
        part = lax.dynamic_index_in_dim(by_group, (y + d) % n_y, 0, keepdims=False)
        if d > 0:
            part = lax.ppermute(part, "y", [(a, (a + d) % n_y) for a in range(n_y)])
        parts.append(part)
    q_in, kv = lax.optimization_barrier((jnp.stack(parts, axis=1), kv))
    q = lax.all_to_all(q_in, "z", split_axis=0, concat_axis=0, tiled=True)

    x_axes = ("x_lo", "x_hi")
    pieces = []
    for piece in [kv] + [lax.ppermute(kv, x_axes, ring(step)) for step in (-1, 2, 1)]:
        pieces += [piece, lax.ppermute(piece, "core", [(0, 1), (1, 0)])]
    place = jnp.stack([lax.axis_index(name) for name in ("x_lo", "x_hi", "core", "y")])
    out = attend(place.astype(jnp.int32), span_mask, span_counts, q, pieces)
    back = exchange(out)
    return back.transpose(1, 0, 2).reshape(1, tok_rows, width)


def solution(mesh):
    fine = Mesh(mesh.devices.reshape(4, 2, 2, 16, 2), ("y", "x_lo", "x_hi", "z", "core"))
    split = P(("y", "x_lo"), ("x_hi", "z", "core"), None)
    return jax.shard_map(
        per_device,
        mesh=fine,
        in_specs=(split, split, split, P(), P()),
        out_specs=split,
        check_vma=False,
    )
```

```python
import jax
import jax.numpy as jnp
from jax import lax
from jax.experimental import pallas as pl
from jax.experimental.pallas import tpu as pltpu
from jax.sharding import Mesh, PartitionSpec as P

HD = 128
LOW = -1e30
LOG2E = 1.4426950408889634
UNROLL = 2


def attend_kernel(place, mask, counts, q_ref, *rest):
    pieces = rest[:8]
    out_ref, k_buf, v_buf = rest[8:11]
    scores, row_tops = rest[11 : 11 + 2 * UNROLL], rest[11 + 2 * UNROLL : 11 + 4 * UNROLL]
    acc_ref, top_ref, total_ref, todo, sems = rest[11 + 4 * UNROLL :]
    x_lo, x_hi, core, y = place[0], place[1], place[2], place[3]
    x = x_hi * 2 + x_lo
    copies = {}
    for d in range(4):
        for part, buf in enumerate((k_buf, v_buf)):
            for e in range(2):
                copies[d, e, part] = pltpu.make_async_copy(
                    pieces[2 * d + e].at[:, part],
                    buf.at[d % 2, ((x + d) % 4) // 2, (core + e) % 2],
                    sems.at[2 * d + e, part],
                )
    for side in range(2):
        for part in range(2):
            for d in (side, side + 2):
                for e in range(2):
                    copies[d, e, part].start()

    def wait(side, part):
        for d in (side, side + 2):
            for e in range(2):
                copies[d, e, part].wait()

    def list_block(i, n):
        side, iy, jy = i // 16, i // 4 % 4, i % 4
        todo[n] = i
        return n + mask[iy * 2 + x_lo, jy * 2 + (x_lo + side) % 2]

    first = lax.fori_loop(0, 16, list_block, 0)
    count = lax.fori_loop(16, 32, list_block, first)

    acc_ref[...] = jnp.zeros_like(acc_ref)
    top_ref[...] = jnp.full_like(top_ref, LOW)
    total_ref[...] = jnp.zeros_like(total_ref)
    scale = LOG2E / HD**0.5
    lane = lax.broadcasted_iota(jnp.int32, (1, 128), 1)
    late = 768 + lane // 16 * 32 + lane % 16

    def score(n, slot):
        i = todo[jnp.minimum(n, count - 1)]
        side, iy, jy = i // 16, i // 4 % 4, i % 4
        live = counts[jy * 2 + (x_lo + side) % 2]
        q = q_ref[:, (y + 4 - iy) % 4].reshape(256, HD)
        k = k_buf[side, :, :, pl.ds(jy * 16, 16)].reshape(1024, HD)
        s = lax.dot_general(q, k, (((1,), (1,)), ((), ())), preferred_element_type=jnp.float32)
        top = None
        for g in range(8):
            a = s[:, g * 128 : (g + 1) * 128]
            if g >= 4 and g % 2 == 1:
                a = jnp.where(late + g // 2 % 2 * 16 < live, a, LOW)
            scores[slot][:, g * 128 : (g + 1) * 128] = a
            top = a if top is None else jnp.maximum(top, a)
        row_tops[slot][...] = jnp.broadcast_to(jnp.max(top, axis=1, keepdims=True), (256, 128))

    def mix(n, slot):
        i = todo[jnp.minimum(n, count - 1)]
        side, jy = i // 16, i % 4
        shift = row_tops[slot][...] * scale
        total, weights = None, []
        for g in range(4):
            at = g * 256
            wa = jnp.exp2(scores[slot][:, at : at + 128] * scale - shift)
            wb = jnp.exp2(scores[slot][:, at + 128 : at + 256] * scale - shift)
            w = jnp.concatenate([wa.astype(jnp.bfloat16), wb.astype(jnp.bfloat16)], axis=1)
            weights.append(w)
            total = wa + wb if total is None else total + (wa + wb)
        v = v_buf[side, :, :, pl.ds(jy * 16, 16)].reshape(1024, HD)
        acc = jnp.dot(jnp.concatenate(weights, axis=1), v, preferred_element_type=jnp.float32)
        return row_tops[slot][...], total, acc

    def merge(n, state):
        top, total, acc = state
        iy = todo[jnp.minimum(n, count - 1)] // 4 % 4
        top = jnp.where(n < count, top, LOW)
        old = top_ref[iy]
        new = jnp.maximum(old, top)
        keep, add = jnp.exp2((old - new) * scale), jnp.exp2((top - new) * scale)
        total_ref[iy] = total_ref[iy] * keep + total * add
        acc_ref[iy] = acc_ref[iy] * keep + acc * add
        top_ref[iy] = new

    def step(n, slot):
        @pl.when((n + 2 * UNROLL > first) & (n + UNROLL <= first))
        def _():
            wait(1, 0)
            wait(1, 1)

        for u in range(UNROLL):
            score(n + UNROLL + u, (1 - slot) * UNROLL + u)
        states = [mix(n + u, slot * UNROLL + u) for u in range(UNROLL)]
        for u in range(UNROLL):
            merge(n + u, states[u])

    wait(0, 0)
    for u in range(UNROLL):
        score(u, u)
    wait(0, 1)

    def pair(m, _):
        step(2 * UNROLL * m, 0)

        @pl.when(2 * UNROLL * m + UNROLL < count)
        def _():
            step(2 * UNROLL * m + UNROLL, 1)

        return 0

    lax.fori_loop(0, (count + 2 * UNROLL - 1) // (2 * UNROLL), pair, 0)
    for iy in range(4):
        total = jnp.sum(total_ref[iy], axis=1, keepdims=True)
        out_ref[iy * 16 : (iy + 1) * 16] = (acc_ref[iy] / total).astype(jnp.bfloat16).reshape(16, 16, HD)

def attend(place, mask, counts, q, pieces):
    smem = pl.BlockSpec(memory_space=pltpu.SMEM)
    vmem = pl.BlockSpec(memory_space=pltpu.VMEM)
    return pl.pallas_call(
        attend_kernel,
        out_shape=jax.ShapeDtypeStruct((64, 16, HD), jnp.bfloat16),
        in_specs=[smem, smem, smem, vmem] + [pl.BlockSpec(memory_space=pl.ANY)] * 8,
        out_specs=vmem,
        scratch_shapes=[
            pltpu.VMEM((2, 2, 2, 64, 16, HD), jnp.bfloat16),
            pltpu.VMEM((2, 2, 2, 64, 16, HD), jnp.bfloat16),
            *[pltpu.VMEM((256, 1024), jnp.float32)] * (2 * UNROLL),
            *[pltpu.VMEM((256, HD), jnp.float32)] * (2 * UNROLL),
            pltpu.VMEM((4, 256, HD), jnp.float32),
            pltpu.VMEM((4, 256, HD), jnp.float32),
            pltpu.VMEM((4, 256, HD), jnp.float32),
            pltpu.SMEM((33,), jnp.int32),
            pltpu.SemaphoreType.DMA((8, 2)),
        ],
        compiler_params=pltpu.CompilerParams(vmem_limit_bytes=40 * 1024 * 1024),
        cost_estimate=pl.CostEstimate(
            flops=4 * 1024 * 8192 * HD, bytes_accessed=5 << 20, transcendentals=1024 * 8192
        ),
    )(place, mask, counts, q, *pieces)


def pack_kernel(k_ref, v_ref, out_ref):
    for head in range(out_ref.shape[0]):
        at = head * HD
        out_ref[head, 0] = k_ref[:, at : at + HD]
        out_ref[head, 1] = v_ref[:, at : at + HD]


def pack(keys, values):
    rows, width = keys.shape
    return pl.pallas_call(
        pack_kernel,
        out_shape=jax.ShapeDtypeStruct((width // HD, 2, rows, HD), keys.dtype),
        in_specs=[pl.BlockSpec(memory_space=pltpu.VMEM)] * 2,
        out_specs=pl.BlockSpec(memory_space=pltpu.VMEM),
    )(keys, values)


def ring(step):
    def index(x):
        return (x % 2) * 2 + x // 2

    return [(index(x), index((x + step) % 4)) for x in range(4)]


def per_device(queries, keys, values, span_mask, span_counts):
    tok_rows, width = queries.shape[1], queries.shape[2]
    heads = width // HD

    def by_head(array):
        return array.reshape(tok_rows, heads, HD).transpose(1, 0, 2)

    def exchange(array):
        return lax.all_to_all(array, ("y", "z"), split_axis=0, concat_axis=0, tiled=True)

    kv = exchange(pack(keys[0], values[0]))
    n_y = lax.axis_size("y")
    y = lax.axis_index("y")
    by_group = by_head(queries).reshape(n_y, heads // n_y, tok_rows, HD)
    parts = []
    for d in range(n_y):
        part = lax.dynamic_index_in_dim(by_group, (y + d) % n_y, 0, keepdims=False)
        if d > 0:
            part = lax.ppermute(part, "y", [(a, (a + d) % n_y) for a in range(n_y)])
        parts.append(part)
    q_in, kv = lax.optimization_barrier((jnp.stack(parts, axis=1), kv))
    q = lax.all_to_all(q_in, "z", split_axis=0, concat_axis=0, tiled=True)

    x_axes = ("x_lo", "x_hi")
    pieces = []
    for piece in [kv] + [lax.ppermute(kv, x_axes, ring(step)) for step in (-1, 1, 2)]:
        pieces += [piece, lax.ppermute(piece, "core", [(0, 1), (1, 0)])]
    pieces = pieces[:4] + pieces[6:] + pieces[4:6]
    place = jnp.stack([lax.axis_index(name) for name in ("x_lo", "x_hi", "core", "y")])
    out = attend(place.astype(jnp.int32), span_mask, span_counts, q, pieces)
    back = exchange(out)
    return back.transpose(1, 0, 2).reshape(1, tok_rows, width)


def solution(mesh):
    fine = Mesh(mesh.devices.reshape(4, 2, 2, 16, 2), ("y", "x_lo", "x_hi", "z", "core"))
    split = P(("y", "x_lo"), ("x_hi", "z", "core"), None)
    return jax.shard_map(
        per_device,
        mesh=fine,
        in_specs=(split, split, split, P(), P()),
        out_specs=split,
        check_vma=False,
    )
```

```python
import jax
import jax.numpy as jnp
from jax import lax
from jax.experimental import pallas as pl
from jax.experimental.pallas import tpu as pltpu
from jax.sharding import Mesh, PartitionSpec as P

HD = 128
LOW = -1e30
LOG2E = 1.4426950408889634
UNROLL = 1


def attend_kernel(place, mask, counts, q_ref, *rest):
    pieces = rest[:8]
    out_ref, k_buf, v_buf = rest[8:11]
    scores, row_tops = rest[11 : 11 + 2 * UNROLL], rest[11 + 2 * UNROLL : 11 + 4 * UNROLL]
    acc_ref, top_ref, total_ref, todo, sems = rest[11 + 4 * UNROLL :]
    x, y, core = place[0], place[1], place[2]
    copies = {}
    for d in range(4):
        for part, buf in enumerate((k_buf, v_buf)):
            for e in range(2):
                copies[d, e, part] = pltpu.make_async_copy(
                    pieces[2 * d + e].at[:, :, :, part], buf.at[d, e], sems.at[2 * d + e, part]
                )
    for d in range(4):
        for part in range(2):
            for e in range(2):
                copies[d, e, part].start()

    def wait(d, part):
        for e in range(2):
            copies[d, e, part].wait()

    def list_block(i, n):
        d, rel, x_lo = i // 4, i // 2 % 2, i % 2
        todo[n] = i
        return n + mask[y * 2 + (x + rel) % 2, (y + d) % 4 * 2 + x_lo]

    first = lax.fori_loop(0, 4, list_block, 0)
    count = lax.fori_loop(4, 16, list_block, first)

    acc_ref[...] = jnp.zeros_like(acc_ref)
    top_ref[...] = jnp.full_like(top_ref, LOW)
    total_ref[...] = jnp.zeros_like(total_ref)
    scale = LOG2E / HD**0.5
    lane = lax.broadcasted_iota(jnp.int32, (1, 128), 1)
    slot_at = lane // 16 % 2 * 512 + lane // 32 * 32 + lane % 16

    def score(n, to):
        i = todo[jnp.minimum(n, count - 1)]
        d, rel, x_lo = i // 4, i // 2 % 2, i % 2
        live = counts[(y + d) % 4 * 2 + x_lo]
        q = q_ref[:, :, rel].reshape(512, HD)
        k = k_buf[d, :, :, :, x_lo].reshape(1024, HD)
        s = lax.dot_general(q, k, (((1,), (1,)), ((), ())), preferred_element_type=jnp.float32)
        top = None
        for g in range(8):
            a = s[:, g * 128 : (g + 1) * 128]
            if g % 4 >= 2:
                slot = slot_at + (g % 4 * 128 + (core + g // 4) % 2 * 16)
                a = jnp.where(slot < live, a, LOW)
            scores[to][:, g * 128 : (g + 1) * 128] = a
            top = a if top is None else jnp.maximum(top, a)
        row_tops[to][...] = jnp.broadcast_to(jnp.max(top, axis=1, keepdims=True), (512, 128))

    def mix(n, at):
        i = todo[jnp.minimum(n, count - 1)]
        d, x_lo = i // 4, i % 2
        shift = row_tops[at][...] * scale
        total, weights = None, []
        for g in range(8):
            w = jnp.exp2(scores[at][:, g * 128 : (g + 1) * 128] * scale - shift)
            weights.append(w.astype(jnp.bfloat16))
            total = w if total is None else total + w
        v = v_buf[d, :, :, :, x_lo].reshape(1024, HD)
        acc = jnp.dot(jnp.concatenate(weights, axis=1), v, preferred_element_type=jnp.float32)
        return row_tops[at][...], total, acc

    def merge(n, state):
        top, total, acc = state
        rel = todo[jnp.minimum(n, count - 1)] // 2 % 2
        if UNROLL > 1:
            top = jnp.where(n < count, top, LOW)
        old = top_ref[rel]
        new = jnp.maximum(old, top)
        keep, add = jnp.exp2((old - new) * scale), jnp.exp2((top - new) * scale)
        total_ref[rel] = total_ref[rel] * keep + total * add
        acc_ref[rel] = acc_ref[rel] * keep + acc * add
        top_ref[rel] = new

    def step(n, at):
        @pl.when((n + 2 * UNROLL > first) & (n + UNROLL <= first))
        def _():
            for d in range(1, 4):
                wait(d, 0)
                wait(d, 1)

        for u in range(UNROLL):
            score(n + UNROLL + u, (1 - at) * UNROLL + u)
        states = [mix(n + u, at * UNROLL + u) for u in range(UNROLL)]
        for u in range(UNROLL):
            merge(n + u, states[u])

    wait(0, 0)
    for u in range(UNROLL):
        score(u, u)
    wait(0, 1)

    def pair(m, _):
        step(2 * UNROLL * m, 0)

        @pl.when(2 * UNROLL * m + UNROLL < count)
        def _():
            step(2 * UNROLL * m + UNROLL, 1)

        return 0

    lax.fori_loop(0, (count + 2 * UNROLL - 1) // (2 * UNROLL), pair, 0)
    for rel in range(2):
        total = jnp.sum(total_ref[rel], axis=1, keepdims=True)
        result = (acc_ref[rel] / total).astype(jnp.bfloat16).reshape(16, 2, 16, HD)
        for far in range(2):
            out_ref[:, (x + 4 - rel - 2 * far) % 4] = result[:, far]


def attend(place, mask, counts, q, pieces):
    smem = pl.BlockSpec(memory_space=pltpu.SMEM)
    vmem = pl.BlockSpec(memory_space=pltpu.VMEM)
    return pl.pallas_call(
        attend_kernel,
        out_shape=jax.ShapeDtypeStruct((16, 4, 16, HD), jnp.bfloat16),
        in_specs=[smem, smem, smem, vmem] + [pl.BlockSpec(memory_space=pl.ANY)] * 8,
        out_specs=vmem,
        scratch_shapes=[
            pltpu.VMEM((4, 2, 16, 2, 2, 16, HD), jnp.bfloat16),
            pltpu.VMEM((4, 2, 16, 2, 2, 16, HD), jnp.bfloat16),
            *[pltpu.VMEM((512, 1024), jnp.float32)] * (2 * UNROLL),
            *[pltpu.VMEM((512, HD), jnp.float32)] * (2 * UNROLL),
            pltpu.VMEM((2, 512, HD), jnp.float32),
            pltpu.VMEM((2, 512, HD), jnp.float32),
            pltpu.VMEM((2, 512, HD), jnp.float32),
            pltpu.SMEM((17,), jnp.int32),
            pltpu.SemaphoreType.DMA((8, 2)),
        ],
        compiler_params=pltpu.CompilerParams(vmem_limit_bytes=40 * 1024 * 1024),
        cost_estimate=pl.CostEstimate(
            flops=4 * 1024 * 8192 * HD, bytes_accessed=5 << 20, transcendentals=1024 * 8192
        ),
    )(place, mask, counts, q, *pieces)


def pack_kernel(k_ref, v_ref, out_ref):
    for head in range(out_ref.shape[0]):
        at = head * HD
        out_ref[head, 0] = k_ref[:, at : at + HD]
        out_ref[head, 1] = v_ref[:, at : at + HD]


def pack(keys, values):
    rows, width = keys.shape
    return pl.pallas_call(
        pack_kernel,
        out_shape=jax.ShapeDtypeStruct((width // HD, 2, rows, HD), keys.dtype),
        in_specs=[pl.BlockSpec(memory_space=pltpu.VMEM)] * 2,
        out_specs=pl.BlockSpec(memory_space=pltpu.VMEM),
    )(keys, values)


def ring(step):
    def index(x):
        return (x % 2) * 2 + x // 2

    return [(index(x), index((x + step) % 4)) for x in range(4)]


def per_device(queries, keys, values, span_mask, span_counts):
    tok_rows, width = queries.shape[1], queries.shape[2]
    heads = width // HD

    def by_head(array):
        return array.reshape(tok_rows, heads, HD).transpose(1, 0, 2)

    def exchange(array):
        return lax.all_to_all(
            array, ("z", "x_hi", "x_lo"), split_axis=0, concat_axis=0, tiled=True
        )

    kv = exchange(pack(keys[0], values[0]))
    n_x, n_y = 4, lax.axis_size("y")
    x = lax.axis_index("x_hi") * 2 + lax.axis_index("x_lo")
    by_group = by_head(queries).reshape(heads // n_x, n_x, tok_rows, HD)
    parts = []
    for d in range(n_x):
        part = lax.dynamic_index_in_dim(by_group, (x + d) % n_x, 1, keepdims=False)
        if d > 0:
            part = lax.ppermute(part, ("x_lo", "x_hi"), ring(d))
        parts.append(part)
    q_in, kv = lax.optimization_barrier((jnp.stack(parts, axis=1), kv))
    q = lax.all_to_all(q_in, "z", split_axis=0, concat_axis=0, tiled=True)

    near = [lax.ppermute(kv, "y", [(a, (a - d) % n_y) for a in range(n_y)]) for d in (1, 3, 2)]
    pieces = []
    for piece in (kv, near[0], near[2], near[1]):
        pieces += [piece, lax.ppermute(piece, "core", [(0, 1), (1, 0)])]
    place = jnp.stack([x, lax.axis_index("y"), lax.axis_index("core")])
    out = attend(
        place.astype(jnp.int32),
        span_mask,
        span_counts,
        q.reshape(16, 2, 2, tok_rows, HD),
        [piece.reshape(16, 2, 2, 2, tok_rows, HD) for piece in pieces],
    )
    back = exchange(out.reshape(heads, tok_rows, HD))
    return back.transpose(1, 0, 2).reshape(1, tok_rows, width)


def solution(mesh):
    fine = Mesh(mesh.devices.reshape(4, 2, 2, 16, 2), ("y", "x_lo", "x_hi", "z", "core"))
    split = P(("y", "x_lo"), ("x_hi", "z", "core"), None)
    return jax.shard_map(
        per_device,
        mesh=fine,
        in_specs=(split, split, split, P(), P()),
        out_specs=split,
        check_vma=False,
    )
```

```python
import jax
import jax.numpy as jnp
from jax import lax
from jax.experimental import pallas as pl
from jax.experimental.pallas import tpu as pltpu
from jax.sharding import Mesh, PartitionSpec as P

HD = 128
LOW = -1e30
LOG2E = 1.4426950408889634
UNROLL = 2


def attend_kernel(place, mask, counts, q_ref, *rest):
    pieces = rest[:8]
    out_ref, k_buf, v_buf = rest[8:11]
    scores, row_tops = rest[11 : 11 + 2 * UNROLL], rest[11 + 2 * UNROLL : 11 + 4 * UNROLL]
    acc_ref, top_ref, total_ref, todo, sems = rest[11 + 4 * UNROLL :]
    x_lo, x_hi, core, y = place[0], place[1], place[2], place[3]
    x = x_hi * 2 + x_lo
    copies = {}
    for d in range(4):
        for part, buf in enumerate((k_buf, v_buf)):
            for e in range(2):
                copies[d, e, part] = pltpu.make_async_copy(
                    pieces[2 * d + e].at[:, :, part],
                    buf.at[d % 2, ((x + d) % 4) // 2, (core + e) % 2],
                    sems.at[2 * d + e, part],
                )
    for side in range(2):
        for part in range(2):
            for d in (side, side + 2):
                for e in range(2):
                    copies[d, e, part].start()

    def wait(side, part):
        for d in (side, side + 2):
            for e in range(2):
                copies[d, e, part].wait()

    def list_block(i, n):
        side, iy, jy = i // 16, i // 4 % 4, i % 4
        todo[n] = i
        return n + mask[iy * 2 + x_lo, jy * 2 + (x_lo + side) % 2]

    first = lax.fori_loop(0, 16, list_block, 0)
    count = lax.fori_loop(16, 32, list_block, first)

    acc_ref[...] = jnp.zeros_like(acc_ref)
    top_ref[...] = jnp.full_like(top_ref, LOW)
    total_ref[...] = jnp.zeros_like(total_ref)
    scale = LOG2E / HD**0.5
    lane = lax.broadcasted_iota(jnp.int32, (1, 128), 1)
    late = 768 + lane // 16 * 32 + lane % 16

    def score(n, slot):
        i = todo[jnp.minimum(n, count - 1)]
        side, iy, jy = i // 16, i // 4 % 4, i % 4
        live = counts[jy * 2 + (x_lo + side) % 2]
        q = q_ref[:, (y + 4 - iy) % 4].reshape(256, HD)
        k = k_buf[side, :, :, :, jy].reshape(1024, HD)
        s = lax.dot_general(q, k, (((1,), (1,)), ((), ())), preferred_element_type=jnp.float32)
        top = None
        for g in range(8):
            a = s[:, g * 128 : (g + 1) * 128]
            if g >= 4 and g % 2 == 1:
                a = jnp.where(late + g // 2 % 2 * 16 < live, a, LOW)
            scores[slot][:, g * 128 : (g + 1) * 128] = a
            top = a if top is None else jnp.maximum(top, a)
        row_tops[slot][...] = jnp.broadcast_to(jnp.max(top, axis=1, keepdims=True), (256, 128))

    def mix(n, slot):
        i = todo[jnp.minimum(n, count - 1)]
        side, jy = i // 16, i % 4
        shift = row_tops[slot][...] * scale
        total, weights = None, []
        for g in range(4):
            at = g * 256
            wa = jnp.exp2(scores[slot][:, at : at + 128] * scale - shift)
            wb = jnp.exp2(scores[slot][:, at + 128 : at + 256] * scale - shift)
            w = jnp.concatenate([wa.astype(jnp.bfloat16), wb.astype(jnp.bfloat16)], axis=1)
            weights.append(w)
            total = wa + wb if total is None else total + (wa + wb)
        v = v_buf[side, :, :, :, jy].reshape(1024, HD)
        acc = jnp.dot(jnp.concatenate(weights, axis=1), v, preferred_element_type=jnp.float32)
        return row_tops[slot][...], total, acc

    def merge(n, state):
        top, total, acc = state
        iy = todo[jnp.minimum(n, count - 1)] // 4 % 4
        top = jnp.where(n < count, top, LOW)
        old = top_ref[iy]
        new = jnp.maximum(old, top)
        keep, add = jnp.exp2((old - new) * scale), jnp.exp2((top - new) * scale)
        total_ref[iy] = total_ref[iy] * keep + total * add
        acc_ref[iy] = acc_ref[iy] * keep + acc * add
        top_ref[iy] = new

    def step(n, slot):
        @pl.when((n + 2 * UNROLL > first) & (n + UNROLL <= first))
        def _():
            wait(1, 0)
            wait(1, 1)

        for u in range(UNROLL):
            score(n + UNROLL + u, (1 - slot) * UNROLL + u)
        states = [mix(n + u, slot * UNROLL + u) for u in range(UNROLL)]
        for u in range(UNROLL):
            merge(n + u, states[u])

    wait(0, 0)
    for u in range(UNROLL):
        score(u, u)
    wait(0, 1)

    def pair(m, _):
        step(2 * UNROLL * m, 0)

        @pl.when(2 * UNROLL * m + UNROLL < count)
        def _():
            step(2 * UNROLL * m + UNROLL, 1)

        return 0

    lax.fori_loop(0, (count + 2 * UNROLL - 1) // (2 * UNROLL), pair, 0)
    for iy in range(4):
        total = jnp.sum(total_ref[iy], axis=1, keepdims=True)
        out_ref[:, iy] = (acc_ref[iy] / total).astype(jnp.bfloat16).reshape(16, 16, HD)

def attend(place, mask, counts, q, pieces):
    smem = pl.BlockSpec(memory_space=pltpu.SMEM)
    vmem = pl.BlockSpec(memory_space=pltpu.VMEM)
    return pl.pallas_call(
        attend_kernel,
        out_shape=jax.ShapeDtypeStruct((16, 4, 16, HD), jnp.bfloat16),
        in_specs=[smem, smem, smem, vmem] + [pl.BlockSpec(memory_space=pl.ANY)] * 8,
        out_specs=vmem,
        scratch_shapes=[
            pltpu.VMEM((2, 2, 2, 16, 4, 16, HD), jnp.bfloat16),
            pltpu.VMEM((2, 2, 2, 16, 4, 16, HD), jnp.bfloat16),
            *[pltpu.VMEM((256, 1024), jnp.float32)] * (2 * UNROLL),
            *[pltpu.VMEM((256, HD), jnp.float32)] * (2 * UNROLL),
            pltpu.VMEM((4, 256, HD), jnp.float32),
            pltpu.VMEM((4, 256, HD), jnp.float32),
            pltpu.VMEM((4, 256, HD), jnp.float32),
            pltpu.SMEM((33,), jnp.int32),
            pltpu.SemaphoreType.DMA((8, 2)),
        ],
        compiler_params=pltpu.CompilerParams(vmem_limit_bytes=40 * 1024 * 1024),
        cost_estimate=pl.CostEstimate(
            flops=4 * 1024 * 8192 * HD, bytes_accessed=5 << 20, transcendentals=1024 * 8192
        ),
    )(place, mask, counts, q, *pieces)


def pack_kernel(k_ref, v_ref, out_ref):
    for head in range(out_ref.shape[0]):
        at = head * HD
        out_ref[head, 0] = k_ref[:, at : at + HD]
        out_ref[head, 1] = v_ref[:, at : at + HD]


def pack(keys, values):
    rows, width = keys.shape
    return pl.pallas_call(
        pack_kernel,
        out_shape=jax.ShapeDtypeStruct((width // HD, 2, rows, HD), keys.dtype),
        in_specs=[pl.BlockSpec(memory_space=pltpu.VMEM)] * 2,
        out_specs=pl.BlockSpec(memory_space=pltpu.VMEM),
    )(keys, values)


def ring(step):
    def index(x):
        return (x % 2) * 2 + x // 2

    return [(index(x), index((x + step) % 4)) for x in range(4)]


def per_device(queries, keys, values, span_mask, span_counts):
    tok_rows, width = queries.shape[1], queries.shape[2]
    heads = width // HD

    def by_head(array):
        return array.reshape(tok_rows, heads, HD).transpose(1, 0, 2)

    def exchange(array):
        return lax.all_to_all(array, ("z", "y"), split_axis=0, concat_axis=0, tiled=True)

    kv = exchange(pack(keys[0], values[0]))
    n_y = lax.axis_size("y")
    y = lax.axis_index("y")
    by_group = by_head(queries).reshape(heads // n_y, n_y, tok_rows, HD)
    parts = []
    for d in range(n_y):
        part = lax.dynamic_index_in_dim(by_group, (y + d) % n_y, 1, keepdims=False)
        if d > 0:
            part = lax.ppermute(part, "y", [(a, (a + d) % n_y) for a in range(n_y)])
        parts.append(part)
    q_in, kv = lax.optimization_barrier((jnp.stack(parts, axis=1), kv))
    q = lax.all_to_all(q_in, "z", split_axis=0, concat_axis=0, tiled=True)

    x_axes = ("x_lo", "x_hi")
    pieces = []
    for piece in [kv] + [lax.ppermute(kv, x_axes, ring(step)) for step in (-1, 1, 2)]:
        pieces += [piece, lax.ppermute(piece, "core", [(0, 1), (1, 0)])]
    pieces = pieces[:4] + pieces[6:] + pieces[4:6]
    pieces = [piece.reshape(heads // n_y, n_y, 2, tok_rows, HD) for piece in pieces]
    place = jnp.stack([lax.axis_index(name) for name in ("x_lo", "x_hi", "core", "y")])
    out = attend(place.astype(jnp.int32), span_mask, span_counts, q, pieces)
    back = exchange(out.reshape(heads, tok_rows, HD))
    return back.transpose(1, 0, 2).reshape(1, tok_rows, width)


def solution(mesh):
    fine = Mesh(mesh.devices.reshape(4, 2, 2, 16, 2), ("y", "x_lo", "x_hi", "z", "core"))
    split = P(("y", "x_lo"), ("x_hi", "z", "core"), None)
    return jax.shard_map(
        per_device,
        mesh=fine,
        in_specs=(split, split, split, P(), P()),
        out_specs=split,
        check_vma=False,
    )
```

```python
import jax
import jax.numpy as jnp
from jax import lax
from jax.experimental import pallas as pl
from jax.experimental.pallas import tpu as pltpu
from jax.sharding import Mesh, PartitionSpec as P

HD = 128
LOW = -1e30
LOG2E = 1.4426950408889634
UNROLL = 1


def attend_kernel(place, mask, counts, q_ref, *rest):
    pieces = rest[:8]
    out_ref, q_buf, k_buf, v_buf = rest[8:12]
    scores, row_tops = rest[12 : 12 + 2 * UNROLL], rest[12 + 2 * UNROLL : 12 + 4 * UNROLL]
    acc_ref, top_ref, total_ref, todo, sems, q_sem = rest[12 + 4 * UNROLL :]
    x_lo, x_hi, core, y = place[0], place[1], place[2], place[3]
    q_copy = pltpu.make_async_copy(q_ref, q_buf, q_sem)
    q_copy.start()
    copies = {}
    for d in range(4):
        for part, buf in enumerate((k_buf, v_buf)):
            for e in range(2):
                copies[d, e, part] = pltpu.make_async_copy(
                    pieces[2 * d + e].at[:, part],
                    buf.at[d % 2, x_hi ^ (d // 2), core ^ e],
                    sems.at[2 * d + e, part],
                )
    for side in range(2):
        for part in range(2):
            for d in (side, side + 2):
                for e in range(2):
                    copies[d, e, part].start()

    def wait(side, part):
        for d in (side, side + 2):
            for e in range(2):
                copies[d, e, part].wait()

    def list_block(i, n):
        side, iy, jy = i // 16, i // 4 % 4, i % 4
        todo[n] = i
        return n + mask[iy * 2 + x_lo, jy * 2 + (x_lo + side) % 2]

    first = lax.fori_loop(0, 16, list_block, 0)
    count = lax.fori_loop(16, 32, list_block, first)

    acc_ref[...] = jnp.zeros_like(acc_ref)
    top_ref[...] = jnp.full_like(top_ref, LOW)
    total_ref[...] = jnp.zeros_like(total_ref)
    scale = LOG2E / HD**0.5
    row = lax.broadcasted_iota(jnp.int32, (128, 256), 0)
    late = 768 + row // 16 * 32 + row % 16

    def score(n, slot):
        i = todo[jnp.minimum(n, count - 1)]
        side, iy, jy = i // 16, i // 4 % 4, i % 4
        live = counts[jy * 2 + (x_lo + side) % 2]
        q = q_buf[:, y ^ iy].reshape(256, HD)
        k = k_buf[side, :, :, pl.ds(jy * 16, 16)].reshape(1024, HD)
        s = lax.dot_general(k, q, (((1,), (1,)), ((), ())), preferred_element_type=jnp.float32)
        top = None
        for g in range(8):
            a = s[g * 128 : (g + 1) * 128]
            if g >= 4 and g % 2 == 1:
                a = jnp.where(late + g // 2 % 2 * 16 < live, a, LOW)
            scores[slot][g * 128 : (g + 1) * 128] = a
            top = a if top is None else jnp.maximum(top, a)
        row_tops[slot][...] = jnp.broadcast_to(jnp.max(top, axis=0, keepdims=True), (8, 256))

    def mix(n, slot):
        i = todo[jnp.minimum(n, count - 1)]
        side, jy = i // 16, i % 4
        shift = row_tops[slot][:1] * scale
        total, weights = None, []
        for g in range(8):
            w = jnp.exp2(scores[slot][g * 128 : (g + 1) * 128] * scale - shift)
            weights.append(w.astype(jnp.bfloat16))
            total = w if total is None else total + w
        total = jnp.sum(total, axis=0, keepdims=True)
        v = v_buf[side, :, :, pl.ds(jy * 16, 16)].reshape(1024, HD)
        weights = jnp.concatenate(weights, axis=0)
        acc = lax.dot_general(
            v, weights, (((0,), (0,)), ((), ())), preferred_element_type=jnp.float32
        )
        return row_tops[slot][:1], total, acc

    def merge(n, state):
        top, total, acc = state
        iy = todo[jnp.minimum(n, count - 1)] // 4 % 4
        top = jnp.where(n < count, top, LOW)
        old = top_ref[iy][:1]
        new = jnp.maximum(old, top)
        keep, add = jnp.exp2((old - new) * scale), jnp.exp2((top - new) * scale)
        total_ref[iy] = jnp.broadcast_to(total_ref[iy][:1] * keep + total * add, (8, 256))
        acc_ref[iy] = acc_ref[iy] * keep + acc * add
        top_ref[iy] = jnp.broadcast_to(new, (8, 256))

    def step(n, slot):
        @pl.when((n + 2 * UNROLL > first) & (n + UNROLL <= first))
        def _():
            wait(1, 0)
            wait(1, 1)

        for u in range(UNROLL):
            score(n + UNROLL + u, (1 - slot) * UNROLL + u)
        states = [mix(n + u, slot * UNROLL + u) for u in range(UNROLL)]
        for u in range(UNROLL):
            merge(n + u, states[u])

    q_copy.wait()
    wait(0, 0)
    for u in range(UNROLL):
        score(u, u)
    wait(0, 1)

    def pair(m, _):
        step(2 * UNROLL * m, 0)

        @pl.when(2 * UNROLL * m + UNROLL < count)
        def _():
            step(2 * UNROLL * m + UNROLL, 1)

        return 0

    lax.fori_loop(0, (count + 2 * UNROLL - 1) // (2 * UNROLL), pair, 0)
    for iy in range(4):
        result = (acc_ref[iy] / total_ref[iy][:1]).T.astype(jnp.bfloat16)
        out_ref[iy * 16 : (iy + 1) * 16] = result.reshape(16, 16, HD)


def attend(place, mask, counts, q, pieces):
    smem = pl.BlockSpec(memory_space=pltpu.SMEM)
    vmem = pl.BlockSpec(memory_space=pltpu.VMEM)
    return pl.pallas_call(
        attend_kernel,
        out_shape=jax.ShapeDtypeStruct((64, 16, HD), jnp.bfloat16),
        in_specs=[smem, smem, smem] + [pl.BlockSpec(memory_space=pl.ANY)] * 9,
        out_specs=vmem,
        scratch_shapes=[
            pltpu.VMEM(q.shape, jnp.bfloat16),
            pltpu.VMEM((2, 2, 2, 64, 16, HD), jnp.bfloat16),
            pltpu.VMEM((2, 2, 2, 64, 16, HD), jnp.bfloat16),
            *[pltpu.VMEM((1024, 256), jnp.float32)] * (2 * UNROLL),
            *[pltpu.VMEM((8, 256), jnp.float32)] * (2 * UNROLL),
            pltpu.VMEM((4, HD, 256), jnp.float32),
            pltpu.VMEM((4, 8, 256), jnp.float32),
            pltpu.VMEM((4, 8, 256), jnp.float32),
            pltpu.SMEM((33,), jnp.int32),
            pltpu.SemaphoreType.DMA((8, 2)),
            pltpu.SemaphoreType.DMA(()),
        ],
        compiler_params=pltpu.CompilerParams(vmem_limit_bytes=40 * 1024 * 1024),
        cost_estimate=pl.CostEstimate(
            flops=4 * 1024 * 8192 * HD, bytes_accessed=5 << 20, transcendentals=1024 * 8192
        ),
    )(place, mask, counts, q, *pieces)


def pack_kernel(k_ref, v_ref, out_ref):
    for head in range(out_ref.shape[0]):
        at = head * HD
        out_ref[head, 0] = k_ref[:, at : at + HD]
        out_ref[head, 1] = v_ref[:, at : at + HD]


def pack(keys, values):
    rows, width = keys.shape
    return pl.pallas_call(
        pack_kernel,
        out_shape=jax.ShapeDtypeStruct((width // HD, 2, rows, HD), keys.dtype),
        in_specs=[pl.BlockSpec(memory_space=pltpu.VMEM)] * 2,
        out_specs=pl.BlockSpec(memory_space=pltpu.VMEM),
    )(keys, values)


def x_pairs(flip):
    def index(x):
        return x % 2 * 2 + x // 2

    return [(index(x), index(x ^ flip)) for x in range(4)]


def per_device(queries, keys, values, span_mask, span_counts):
    tok_rows, width = queries.shape[1], queries.shape[2]
    heads = width // HD

    def by_head(array):
        return array.reshape(tok_rows, heads, HD).transpose(1, 0, 2)

    def exchange(array):
        return lax.all_to_all(array, ("y", "z"), split_axis=0, concat_axis=0, tiled=True)

    kv = exchange(pack(keys[0], values[0]))
    n_y = lax.axis_size("y")
    y = lax.axis_index("y")
    by_group = by_head(queries).reshape(n_y, heads // n_y, tok_rows, HD)
    parts = []
    for d in range(n_y):
        part = lax.dynamic_index_in_dim(by_group, y ^ d, 0, keepdims=False)
        if d > 0:
            part = lax.ppermute(part, "y", [(a, a ^ d) for a in range(n_y)])
        parts.append(part)
    q_in, kv = lax.optimization_barrier((jnp.stack(parts, axis=1), kv))
    q = lax.all_to_all(q_in, "z", split_axis=0, concat_axis=0, tiled=True)

    x_axes = ("x_lo", "x_hi")
    pieces = []
    for piece in [kv] + [lax.ppermute(kv, x_axes, x_pairs(flip)) for flip in (1, 3, 2)]:
        pieces += [piece, lax.ppermute(piece, "core", [(0, 1), (1, 0)])]
    pieces = pieces[:4] + pieces[6:] + pieces[4:6]
    place = jnp.stack([lax.axis_index(name) for name in ("x_lo", "x_hi", "core", "y")])
    out = attend(place.astype(jnp.int32), span_mask, span_counts, q, pieces)
    back = exchange(out)
    return back.transpose(1, 0, 2).reshape(1, tok_rows, width)


def solution(mesh):
    fine = Mesh(mesh.devices.reshape(4, 2, 2, 16, 2), ("y", "x_lo", "x_hi", "z", "core"))
    split = P(("y", "x_lo"), ("x_hi", "z", "core"), None)
    return jax.shard_map(
        per_device,
        mesh=fine,
        in_specs=(split, split, split, P(), P()),
        out_specs=split,
        check_vma=False,
    )
```

```python
import jax
import jax.numpy as jnp
from jax import lax
from jax.experimental import pallas as pl
from jax.experimental.pallas import tpu as pltpu
from jax.sharding import Mesh, PartitionSpec as P

HD = 128
LOW = -1e30
LOG2E = 1.4426950408889634
UNROLL = 1


def attend_kernel(place, mask, counts, q_ref, *rest):
    pieces = rest[:8]
    out_ref, q_buf, k_buf, v_buf = rest[8:12]
    scores, row_tops = rest[12 : 12 + 2 * UNROLL], rest[12 + 2 * UNROLL : 12 + 4 * UNROLL]
    acc_ref, top_ref, total_ref, todo, sems, q_sem = rest[12 + 4 * UNROLL :]
    x_lo, x_hi, core, y = place[0], place[1], place[2], place[3]
    q_copy = pltpu.make_async_copy(q_ref, q_buf, q_sem)
    q_copy.start()
    copies = {}
    for d in range(4):
        for part, buf in enumerate((k_buf, v_buf)):
            for e in range(2):
                copies[d, e, part] = pltpu.make_async_copy(
                    pieces[2 * d + e].at[:, part],
                    buf.at[d % 2, (x_hi * 2 + x_lo + d) % 4 // 2, core ^ e],
                    sems.at[2 * d + e, part],
                )
    for side in range(2):
        for part in range(2):
            for d in (side, side + 2):
                for e in range(2):
                    copies[d, e, part].start()

    def wait(side, part):
        for d in (side, side + 2):
            for e in range(2):
                copies[d, e, part].wait()

    def list_block(i, n):
        side, iy, jy = i // 16, i // 4 % 4, i % 4
        todo[n] = i
        return n + mask[iy * 2 + x_lo, jy * 2 + (x_lo + side) % 2]

    first = lax.fori_loop(0, 16, list_block, 0)
    count = lax.fori_loop(16, 32, list_block, first)

    acc_ref[...] = jnp.zeros_like(acc_ref)
    top_ref[...] = jnp.full_like(top_ref, LOW)
    total_ref[...] = jnp.zeros_like(total_ref)
    scale = LOG2E / HD**0.5
    row = lax.broadcasted_iota(jnp.int32, (128, 256), 0)
    late = 768 + row // 16 * 32 + row % 16

    def score(n, slot):
        i = todo[jnp.minimum(n, count - 1)]
        side, iy, jy = i // 16, i // 4 % 4, i % 4
        live = counts[jy * 2 + (x_lo + side) % 2]
        q = q_buf[:, y ^ iy].reshape(256, HD)
        k = k_buf[side, :, :, pl.ds(jy * 16, 16)].reshape(1024, HD)
        s = lax.dot_general(k, q, (((1,), (1,)), ((), ())), preferred_element_type=jnp.float32)
        top = None
        for g in range(8):
            a = s[g * 128 : (g + 1) * 128]
            if g >= 4 and g % 2 == 1:
                a = jnp.where(late + g // 2 % 2 * 16 < live, a, LOW)
            scores[slot][g * 128 : (g + 1) * 128] = a
            top = a if top is None else jnp.maximum(top, a)
        row_tops[slot][...] = jnp.broadcast_to(jnp.max(top, axis=0, keepdims=True), (8, 256))

    def mix(n, slot):
        i = todo[jnp.minimum(n, count - 1)]
        side, jy = i // 16, i % 4
        shift = row_tops[slot][:1] * scale
        total, weights = None, []
        for g in range(8):
            w = jnp.exp2(scores[slot][g * 128 : (g + 1) * 128] * scale - shift)
            weights.append(w.astype(jnp.bfloat16))
            total = w if total is None else total + w
        total = jnp.sum(total, axis=0, keepdims=True)
        v = v_buf[side, :, :, pl.ds(jy * 16, 16)].reshape(1024, HD)
        weights = jnp.concatenate(weights, axis=0)
        acc = lax.dot_general(
            v, weights, (((0,), (0,)), ((), ())), preferred_element_type=jnp.float32
        )
        return row_tops[slot][:1], total, acc

    def merge(n, state):
        top, total, acc = state
        iy = todo[jnp.minimum(n, count - 1)] // 4 % 4
        top = jnp.where(n < count, top, LOW)
        old = top_ref[iy][:1]
        new = jnp.maximum(old, top)
        keep, add = jnp.exp2((old - new) * scale), jnp.exp2((top - new) * scale)
        total_ref[iy] = jnp.broadcast_to(total_ref[iy][:1] * keep + total * add, (8, 256))
        acc_ref[iy] = acc_ref[iy] * keep + acc * add
        top_ref[iy] = jnp.broadcast_to(new, (8, 256))

    def step(n, slot):
        @pl.when((n + 2 * UNROLL > first) & (n + UNROLL <= first))
        def _():
            wait(1, 0)
            wait(1, 1)

        for u in range(UNROLL):
            score(n + UNROLL + u, (1 - slot) * UNROLL + u)
        states = [mix(n + u, slot * UNROLL + u) for u in range(UNROLL)]
        for u in range(UNROLL):
            merge(n + u, states[u])

    q_copy.wait()
    wait(0, 0)
    for u in range(UNROLL):
        score(u, u)
    wait(0, 1)

    def pair(m, _):
        step(2 * UNROLL * m, 0)

        @pl.when(2 * UNROLL * m + UNROLL < count)
        def _():
            step(2 * UNROLL * m + UNROLL, 1)

        return 0

    lax.fori_loop(0, (count + 2 * UNROLL - 1) // (2 * UNROLL), pair, 0)
    for iy in range(4):
        result = (acc_ref[iy] / total_ref[iy][:1]).T.astype(jnp.bfloat16)
        out_ref[iy * 16 : (iy + 1) * 16] = result.reshape(16, 16, HD)


def attend(place, mask, counts, q, pieces):
    smem = pl.BlockSpec(memory_space=pltpu.SMEM)
    vmem = pl.BlockSpec(memory_space=pltpu.VMEM)
    return pl.pallas_call(
        attend_kernel,
        out_shape=jax.ShapeDtypeStruct((64, 16, HD), jnp.bfloat16),
        in_specs=[smem, smem, smem] + [pl.BlockSpec(memory_space=pl.ANY)] * 9,
        out_specs=vmem,
        scratch_shapes=[
            pltpu.VMEM(q.shape, jnp.bfloat16),
            pltpu.VMEM((2, 2, 2, 64, 16, HD), jnp.bfloat16),
            pltpu.VMEM((2, 2, 2, 64, 16, HD), jnp.bfloat16),
            *[pltpu.VMEM((1024, 256), jnp.float32)] * (2 * UNROLL),
            *[pltpu.VMEM((8, 256), jnp.float32)] * (2 * UNROLL),
            pltpu.VMEM((4, HD, 256), jnp.float32),
            pltpu.VMEM((4, 8, 256), jnp.float32),
            pltpu.VMEM((4, 8, 256), jnp.float32),
            pltpu.SMEM((33,), jnp.int32),
            pltpu.SemaphoreType.DMA((8, 2)),
            pltpu.SemaphoreType.DMA(()),
        ],
        compiler_params=pltpu.CompilerParams(vmem_limit_bytes=40 * 1024 * 1024),
        cost_estimate=pl.CostEstimate(
            flops=4 * 1024 * 8192 * HD, bytes_accessed=5 << 20, transcendentals=1024 * 8192
        ),
    )(place, mask, counts, q, *pieces)


def pack_kernel(k_ref, v_ref, out_ref):
    for head in range(out_ref.shape[0]):
        at = head * HD
        out_ref[head, 0] = k_ref[:, at : at + HD]
        out_ref[head, 1] = v_ref[:, at : at + HD]


def pack(keys, values):
    rows, width = keys.shape
    return pl.pallas_call(
        pack_kernel,
        out_shape=jax.ShapeDtypeStruct((width // HD, 2, rows, HD), keys.dtype),
        in_specs=[pl.BlockSpec(memory_space=pltpu.VMEM)] * 2,
        out_specs=pl.BlockSpec(memory_space=pltpu.VMEM),
    )(keys, values)


def ring(step):
    def index(x):
        return x % 2 * 2 + x // 2

    return [(index(x), index((x + step) % 4)) for x in range(4)]


def per_device(queries, keys, values, span_mask, span_counts):
    tok_rows, width = queries.shape[1], queries.shape[2]
    heads = width // HD

    def by_head(array):
        return array.reshape(tok_rows, heads, HD).transpose(1, 0, 2)

    def exchange(array):
        return lax.all_to_all(array, ("y", "z"), split_axis=0, concat_axis=0, tiled=True)

    kv = exchange(pack(keys[0], values[0]))
    n_y = lax.axis_size("y")
    y = lax.axis_index("y")
    by_group = by_head(queries).reshape(n_y, heads // n_y, tok_rows, HD)
    parts = []
    for d in range(n_y):
        part = lax.dynamic_index_in_dim(by_group, y ^ d, 0, keepdims=False)
        if d > 0:
            part = lax.ppermute(part, "y", [(a, a ^ d) for a in range(n_y)])
        parts.append(part)
    q_in, kv = lax.optimization_barrier((jnp.stack(parts, axis=1), kv))
    q = lax.all_to_all(q_in, "z", split_axis=0, concat_axis=0, tiled=True)

    x_axes = ("x_lo", "x_hi")
    pieces = []
    for piece in [kv] + [lax.ppermute(kv, x_axes, ring(step)) for step in (-1, 1, 2)]:
        pieces += [piece, lax.ppermute(piece, "core", [(0, 1), (1, 0)])]
    pieces = pieces[:4] + pieces[6:] + pieces[4:6]
    place = jnp.stack([lax.axis_index(name) for name in ("x_lo", "x_hi", "core", "y")])
    out = attend(place.astype(jnp.int32), span_mask, span_counts, q, pieces)
    back = exchange(out)
    return back.transpose(1, 0, 2).reshape(1, tok_rows, width)


def solution(mesh):
    fine = Mesh(mesh.devices.reshape(4, 2, 2, 16, 2), ("y", "x_lo", "x_hi", "z", "core"))
    split = P(("y", "x_lo"), ("x_hi", "z", "core"), None)
    return jax.shard_map(
        per_device,
        mesh=fine,
        in_specs=(split, split, split, P(), P()),
        out_specs=split,
        check_vma=False,
    )
```

```python
import jax
import jax.numpy as jnp
from jax import lax
from jax.experimental import pallas as pl
from jax.experimental.pallas import tpu as pltpu
from jax.sharding import Mesh, PartitionSpec as P

HD = 128
LOW = -1e30
LOG2E = 1.4426950408889634
UNROLL = 1


def attend_kernel(place, mask, counts, q_ref, *rest):
    pieces = rest[:8]
    out_ref = rest[8]
    scores, row_tops = rest[9 : 9 + 2 * UNROLL], rest[9 + 2 * UNROLL : 9 + 4 * UNROLL]
    acc_ref, top_ref, total_ref, todo = rest[9 + 4 * UNROLL :]
    x_lo, x_hi, core, y = place[0], place[1], place[2], place[3]

    def slab(side, part, jy):
        blocks = [
            pieces[2 * d + e][pl.ds(jy * 16, 16), part].reshape(256, HD)
            for d in (side, side + 2)
            for e in range(2)
        ]
        return jnp.concatenate(blocks, axis=0)

    def list_block(i, n):
        side, iy, jy = i // 16, i // 4 % 4, i % 4
        todo[n] = i
        return n + mask[iy * 2 + x_lo, jy * 2 + (x_lo + side) % 2]

    first = lax.fori_loop(0, 16, list_block, 0)
    count = lax.fori_loop(16, 32, list_block, first)

    acc_ref[...] = jnp.zeros_like(acc_ref)
    top_ref[...] = jnp.full_like(top_ref, LOW)
    total_ref[...] = jnp.zeros_like(total_ref)
    scale = LOG2E / HD**0.5
    row = lax.broadcasted_iota(jnp.int32, (128, 256), 0)
    late = 256 + row // 16 * 32 + row % 16

    def score(n, slot, side, end):
        i = todo[jnp.minimum(n, end - 1)]
        iy, jy = i // 4 % 4, i % 4
        live = counts[jy * 2 + (x_lo + side) % 2]
        q = q_ref[:, y ^ iy].reshape(256, HD)
        s = lax.dot_general(
            slab(side, 0, jy), q, (((1,), (1,)), ((), ())), preferred_element_type=jnp.float32
        )
        top = None
        for g in range(8):
            a = s[g * 128 : (g + 1) * 128]
            if g % 2 == 1:
                hi = (x_hi * 2 + x_lo + side + g // 4 * 2) % 4 // 2
                a = jnp.where(late + (hi * 512 + (core ^ (g // 2 % 2)) * 16) < live, a, LOW)
            scores[slot][g * 128 : (g + 1) * 128] = a
            top = a if top is None else jnp.maximum(top, a)
        row_tops[slot][...] = jnp.broadcast_to(jnp.max(top, axis=0, keepdims=True), (8, 256))

    def mix(n, slot, side):
        shift = row_tops[slot][:1] * scale
        total, weights = None, []
        for g in range(8):
            w = jnp.exp2(scores[slot][g * 128 : (g + 1) * 128] * scale - shift)
            weights.append(w.astype(jnp.bfloat16))
            total = w if total is None else total + w
        total = jnp.sum(total, axis=0, keepdims=True)
        weights = jnp.concatenate(weights, axis=0)
        acc = lax.dot_general(
            slab(side, 1, todo[n] % 4),
            weights,
            (((0,), (0,)), ((), ())),
            preferred_element_type=jnp.float32,
        )
        return row_tops[slot][:1], total, acc

    def merge(n, state):
        top, total, acc = state
        iy = todo[n] // 4 % 4
        old = top_ref[iy][:1]
        new = jnp.maximum(old, top)
        keep, add = jnp.exp2((old - new) * scale), jnp.exp2((top - new) * scale)
        total_ref[iy] = jnp.broadcast_to(total_ref[iy][:1] * keep + total * add, (8, 256))
        acc_ref[iy] = acc_ref[iy] * keep + acc * add
        top_ref[iy] = jnp.broadcast_to(new, (8, 256))

    def run(side, begin, end):
        def step(n, slot):
            score(n + 1, 1 - slot, side, end)
            merge(n, mix(n, slot, side))

        def pair(m, _):
            n = begin + 2 * m
            step(n, 0)

            @pl.when(n + 1 < end)
            def _():
                step(n + 1, 1)

            return 0

        score(begin, 0, side, end)
        lax.fori_loop(0, (end - begin + 1) // 2, pair, 0)

    run(0, 0, first)

    @pl.when(count > first)
    def _():
        run(1, first, count)

    for iy in range(4):
        result = (acc_ref[iy] / total_ref[iy][:1]).T.astype(jnp.bfloat16)
        out_ref[iy * 16 : (iy + 1) * 16] = result.reshape(16, 16, HD)


def attend(place, mask, counts, q, pieces):
    smem = pl.BlockSpec(memory_space=pltpu.SMEM)
    vmem = pl.BlockSpec(memory_space=pltpu.VMEM)
    return pl.pallas_call(
        attend_kernel,
        out_shape=jax.ShapeDtypeStruct((64, 16, HD), jnp.bfloat16),
        in_specs=[smem, smem, smem] + [vmem] * 9,
        out_specs=vmem,
        scratch_shapes=[
            *[pltpu.VMEM((1024, 256), jnp.float32)] * (2 * UNROLL),
            *[pltpu.VMEM((8, 256), jnp.float32)] * (2 * UNROLL),
            pltpu.VMEM((4, HD, 256), jnp.float32),
            pltpu.VMEM((4, 8, 256), jnp.float32),
            pltpu.VMEM((4, 8, 256), jnp.float32),
            pltpu.SMEM((33,), jnp.int32),
        ],
        compiler_params=pltpu.CompilerParams(vmem_limit_bytes=40 * 1024 * 1024),
        cost_estimate=pl.CostEstimate(
            flops=4 * 1024 * 8192 * HD, bytes_accessed=5 << 20, transcendentals=1024 * 8192
        ),
    )(place, mask, counts, q, *pieces)


def pack_kernel(k_ref, v_ref, out_ref):
    for head in range(out_ref.shape[0]):
        at = head * HD
        out_ref[head, 0] = k_ref[:, at : at + HD]
        out_ref[head, 1] = v_ref[:, at : at + HD]


def pack(keys, values):
    rows, width = keys.shape
    return pl.pallas_call(
        pack_kernel,
        out_shape=jax.ShapeDtypeStruct((width // HD, 2, rows, HD), keys.dtype),
        in_specs=[pl.BlockSpec(memory_space=pltpu.VMEM)] * 2,
        out_specs=pl.BlockSpec(memory_space=pltpu.VMEM),
    )(keys, values)


def ring(step):
    def index(x):
        return x % 2 * 2 + x // 2

    return [(index(x), index((x + step) % 4)) for x in range(4)]


def per_device(queries, keys, values, span_mask, span_counts):
    tok_rows, width = queries.shape[1], queries.shape[2]
    heads = width // HD

    def by_head(array):
        return array.reshape(tok_rows, heads, HD).transpose(1, 0, 2)

    def exchange(array):
        return lax.all_to_all(array, ("y", "z"), split_axis=0, concat_axis=0, tiled=True)

    kv = exchange(pack(keys[0], values[0]))
    n_y = lax.axis_size("y")
    y = lax.axis_index("y")
    by_group = by_head(queries).reshape(n_y, heads // n_y, tok_rows, HD)
    parts = []
    for d in range(n_y):
        part = lax.dynamic_index_in_dim(by_group, y ^ d, 0, keepdims=False)
        if d > 0:
            part = lax.ppermute(part, "y", [(a, a ^ d) for a in range(n_y)])
        parts.append(part)
    q_in, kv = lax.optimization_barrier((jnp.stack(parts, axis=1), kv))
    q = lax.all_to_all(q_in, "z", split_axis=0, concat_axis=0, tiled=True)

    x_axes = ("x_lo", "x_hi")
    pieces = []
    for piece in [kv] + [lax.ppermute(kv, x_axes, ring(step)) for step in (-1, 1, 2)]:
        pieces += [piece, lax.ppermute(piece, "core", [(0, 1), (1, 0)])]
    pieces = pieces[:4] + pieces[6:] + pieces[4:6]
    place = jnp.stack([lax.axis_index(name) for name in ("x_lo", "x_hi", "core", "y")])
    out = attend(place.astype(jnp.int32), span_mask, span_counts, q, pieces)
    back = exchange(out)
    return back.transpose(1, 0, 2).reshape(1, tok_rows, width)


def solution(mesh):
    fine = Mesh(mesh.devices.reshape(4, 2, 2, 16, 2), ("y", "x_lo", "x_hi", "z", "core"))
    split = P(("y", "x_lo"), ("x_hi", "z", "core"), None)
    return jax.shard_map(
        per_device,
        mesh=fine,
        in_specs=(split, split, split, P(), P()),
        out_specs=split,
        check_vma=False,
    )
```

```python
import jax
import jax.numpy as jnp
from jax import lax
from jax.experimental import pallas as pl
from jax.experimental.pallas import tpu as pltpu
from jax.sharding import Mesh, PartitionSpec as P

HD = 128
LOW = -1e30
LOG2E = 1.4426950408889634


def attend_kernel(place, mask, counts, q_ref, *rest):
    pieces = rest[:8]
    out_ref = rest[8]
    scores, row_tops = rest[9:12], rest[12:15]
    acc_ref, top_ref, total_ref, todo = rest[15:]
    x_lo, x_hi, core, y = place[0], place[1], place[2], place[3]

    def slab(side, part, jy):
        blocks = [
            pieces[2 * d + e][pl.ds(jy * 16, 16), part].reshape(256, HD)
            for d in (side, side + 2)
            for e in range(2)
        ]
        return jnp.concatenate(blocks, axis=0)

    def list_block(i, n):
        side, iy, jy = i // 16, i // 4 % 4, i % 4
        todo[n] = i
        return n + mask[iy * 2 + x_lo, jy * 2 + (x_lo + side) % 2]

    first = lax.fori_loop(0, 16, list_block, 0)
    count = lax.fori_loop(16, 32, list_block, first)

    acc_ref[...] = jnp.zeros_like(acc_ref)
    top_ref[...] = jnp.full_like(top_ref, LOW)
    total_ref[...] = jnp.zeros_like(total_ref)
    scale = LOG2E / HD**0.5
    row = lax.broadcasted_iota(jnp.int32, (128, 256), 0)
    late = 256 + row // 16 * 32 + row % 16

    def score(n, slot, side, end):
        i = todo[jnp.minimum(n, end - 1)]
        iy, jy = i // 4 % 4, i % 4
        live = counts[jy * 2 + (x_lo + side) % 2]
        q = q_ref[:, y ^ iy].reshape(256, HD)
        s = lax.dot_general(
            slab(side, 0, jy), q, (((1,), (1,)), ((), ())), preferred_element_type=jnp.float32
        )
        top = None
        for g in range(8):
            a = s[g * 128 : (g + 1) * 128]
            if g % 2 == 1:
                hi = (x_hi * 2 + x_lo + side + g // 4 * 2) % 4 // 2
                a = jnp.where(late + (hi * 512 + (core ^ (g // 2 % 2)) * 16) < live, a, LOW)
            scores[slot][g * 128 : (g + 1) * 128] = a
            top = a if top is None else jnp.maximum(top, a)
        row_tops[slot][...] = jnp.broadcast_to(jnp.max(top, axis=0, keepdims=True), (8, 256))

    def mix(n, slot, side):
        shift = row_tops[slot][:1] * scale
        total, weights = None, []
        for g in range(8):
            w = jnp.exp2(scores[slot][g * 128 : (g + 1) * 128] * scale - shift)
            weights.append(w.astype(jnp.bfloat16))
            total = w if total is None else total + w
        total = jnp.sum(total, axis=0, keepdims=True)
        weights = jnp.concatenate(weights, axis=0)
        acc = lax.dot_general(
            slab(side, 1, todo[n] % 4),
            weights,
            (((0,), (0,)), ((), ())),
            preferred_element_type=jnp.float32,
        )
        return row_tops[slot][:1], total, acc

    def merge(n, state):
        top, total, acc = state
        iy = todo[n] // 4 % 4
        old = top_ref[iy][:1]
        new = jnp.maximum(old, top)
        keep, add = jnp.exp2((old - new) * scale), jnp.exp2((top - new) * scale)
        total_ref[iy] = jnp.broadcast_to(total_ref[iy][:1] * keep + total * add, (8, 256))
        acc_ref[iy] = acc_ref[iy] * keep + acc * add
        top_ref[iy] = jnp.broadcast_to(new, (8, 256))

    def run(side, begin, end, ahead):
        last = end - 1

        def step(n, slot):
            score(n + 1, 1 - slot, side, end)
            merge(n, mix(n, slot, side))

        def pair(m, _):
            n = begin + 2 * m
            step(n, 0)

            @pl.when(n + 1 < last)
            def _():
                step(n + 1, 1)

            return 0

        lax.fori_loop(0, (last - begin + 1) // 2, pair, 0)
        for slot in range(2):

            @pl.when((last - begin) % 2 == slot)
            def _():
                ahead()
                merge(last, mix(last, slot, side))

    score(0, 0, 0, first)
    run(0, 0, first, lambda: score(first, 2, 1, first + 1))

    @pl.when(count > first)
    def _():
        score(first + 1, 0, 1, count)
        merge(first, mix(first, 2, 1))

        @pl.when(count > first + 1)
        def _():
            run(1, first + 1, count, lambda: None)

    for iy in range(4):
        result = (acc_ref[iy] / total_ref[iy][:1]).T.astype(jnp.bfloat16)
        out_ref[iy * 16 : (iy + 1) * 16] = result.reshape(16, 16, HD)


def attend(place, mask, counts, q, pieces):
    smem = pl.BlockSpec(memory_space=pltpu.SMEM)
    vmem = pl.BlockSpec(memory_space=pltpu.VMEM)
    return pl.pallas_call(
        attend_kernel,
        out_shape=jax.ShapeDtypeStruct((64, 16, HD), jnp.bfloat16),
        in_specs=[smem, smem, smem] + [vmem] * 9,
        out_specs=vmem,
        scratch_shapes=[
            *[pltpu.VMEM((1024, 256), jnp.float32)] * 3,
            *[pltpu.VMEM((8, 256), jnp.float32)] * 3,
            pltpu.VMEM((4, HD, 256), jnp.float32),
            pltpu.VMEM((4, 8, 256), jnp.float32),
            pltpu.VMEM((4, 8, 256), jnp.float32),
            pltpu.SMEM((33,), jnp.int32),
        ],
        compiler_params=pltpu.CompilerParams(vmem_limit_bytes=40 * 1024 * 1024),
        cost_estimate=pl.CostEstimate(
            flops=4 * 1024 * 8192 * HD, bytes_accessed=5 << 20, transcendentals=1024 * 8192
        ),
    )(place, mask, counts, q, *pieces)


def pack_kernel(k_ref, v_ref, out_ref):
    for head in range(out_ref.shape[0]):
        at = head * HD
        out_ref[head, 0] = k_ref[:, at : at + HD]
        out_ref[head, 1] = v_ref[:, at : at + HD]


def pack(keys, values):
    rows, width = keys.shape
    return pl.pallas_call(
        pack_kernel,
        out_shape=jax.ShapeDtypeStruct((width // HD, 2, rows, HD), keys.dtype),
        in_specs=[pl.BlockSpec(memory_space=pltpu.VMEM)] * 2,
        out_specs=pl.BlockSpec(memory_space=pltpu.VMEM),
    )(keys, values)


def ring(step):
    def index(x):
        return x % 2 * 2 + x // 2

    return [(index(x), index((x + step) % 4)) for x in range(4)]


def per_device(queries, keys, values, span_mask, span_counts):
    tok_rows, width = queries.shape[1], queries.shape[2]
    heads = width // HD

    def by_head(array):
        return array.reshape(tok_rows, heads, HD).transpose(1, 0, 2)

    def exchange(array):
        return lax.all_to_all(array, ("y", "z"), split_axis=0, concat_axis=0, tiled=True)

    kv = exchange(pack(keys[0], values[0]))
    n_y = lax.axis_size("y")
    y = lax.axis_index("y")
    by_group = by_head(queries).reshape(n_y, heads // n_y, tok_rows, HD)
    parts = []
    for d in range(n_y):
        part = lax.dynamic_index_in_dim(by_group, y ^ d, 0, keepdims=False)
        if d > 0:
            part = lax.ppermute(part, "y", [(a, a ^ d) for a in range(n_y)])
        parts.append(part)
    q_in, kv = lax.optimization_barrier((jnp.stack(parts, axis=1), kv))
    q = lax.all_to_all(q_in, "z", split_axis=0, concat_axis=0, tiled=True)

    x_axes = ("x_lo", "x_hi")
    pieces = []
    for piece in [kv] + [lax.ppermute(kv, x_axes, ring(step)) for step in (-1, 1, 2)]:
        pieces += [piece, lax.ppermute(piece, "core", [(0, 1), (1, 0)])]
    pieces = pieces[:4] + pieces[6:] + pieces[4:6]
    place = jnp.stack([lax.axis_index(name) for name in ("x_lo", "x_hi", "core", "y")])
    out = attend(place.astype(jnp.int32), span_mask, span_counts, q, pieces)
    back = exchange(out)
    return back.transpose(1, 0, 2).reshape(1, tok_rows, width)


def solution(mesh):
    fine = Mesh(mesh.devices.reshape(4, 2, 2, 16, 2), ("y", "x_lo", "x_hi", "z", "core"))
    split = P(("y", "x_lo"), ("x_hi", "z", "core"), None)
    return jax.shard_map(
        per_device,
        mesh=fine,
        in_specs=(split, split, split, P(), P()),
        out_specs=split,
        check_vma=False,
    )
```
